256 devices in a mesh: ctx: 64 (over z, y, core), tp: 4 (over x).
Axes of the slice: x: 4, y: 4, z: 8, core: 2. Of those that a mesh axis runs over, the one named last changes fastest.
Arguments:
- ctx_queries: bfloat16 [16384, 8192], P('ctx', 'tp'), may hold values from -16 to 16
- ctx_keys: bfloat16 [16384, 1024], P('ctx', 'tp'), may hold values from -18 to 18
- ctx_values: bfloat16 [16384, 1024], P('ctx', 'tp'), may hold values from -6 to 6
- block_map: int32 [64], replicated, may hold values from 0 to 63, each once
- cache_keys: bfloat16 [16384, 1024], P('ctx', 'tp'), may hold values from -18 to 18
- cache_values: bfloat16 [16384, 1024], P('ctx', 'tp'), may hold values from -6 to 6
- dec_queries: bfloat16 [4, 64, 8192], P(None, 'ctx', 'tp'), may hold values from -16 to 16
- new_keys: bfloat16 [4, 64, 1024], P(None, 'ctx', 'tp'), may hold values from -15 to 15
- new_values: bfloat16 [4, 64, 1024], P(None, 'ctx', 'tp'), may hold values from -6 to 6
- cache_lengths: int32 [64], replicated, may hold values from 2048 to 16384, as said below
- owner: int32 [64], replicated, may hold values from 0 to 63, each once
- out_weight: bfloat16 [8192, 8192], P('tp', 'ctx'), may hold values from -0.0625 to 0.0625
Outputs:
- ctx_out: bfloat16 [16384, 8192], P('ctx', 'tp')
- dec_out: bfloat16 [4, 64, 8192], P(None, 'tp', 'ctx')
The draws below stay inside these ranges and needn't reach their ends.
Inputs may be any that keep to these rules, and one draw needn't show every extreme that they name: `cache_lengths`: one request has the whole cache of 16384 rows valid and one only 2048. `block_map`: each block number once. `owner`: each slot once.
All inputs are finite; a program needn't handle non-finite values.
Results may differ from the reference program's by a relative error of at most 0.005.
Values may be sent and summed in bfloat16 or wider, within the bound.
No kernel may reach another device: no remote copies, remote signals or barrier semaphores. Data moves between devices by JAX's collectives and lax.ppermute only.
A program may use at most 384 MiB of HBM per device.

```python
import math
import jax
import jax.numpy as jnp
from jax import lax

D = 8192
HQ = 64
KV = 8
HD = 128
BLK = 256
CACHE_DEV = 256
STEPS = 4
REQ = 64
CTXTOK = 16384
CACHE = 16384
N_CTX = 64


def draw_ctx_keys(key, part):
    key = jax.random.fold_in(key, 1)
    drawn = jax.random.normal(key, (CTXTOK, KV, HD), jnp.float32) * 3.0
    return jnp.clip(drawn, -18.0, 18.0).reshape(CTXTOK, KV * HD).astype(jnp.bfloat16)


def draw_ctx_queries(key, part):
    key = jax.random.fold_in(key, 2)
    drawn = jax.random.normal(key, (CTXTOK, HQ, HD), jnp.float32)
    return jnp.clip(drawn, -16.0, 16.0).reshape(CTXTOK, HQ * HD).astype(jnp.bfloat16)


def draw_cache_keys(key, part):
    key = jax.random.fold_in(key, 3)
    drawn = jax.random.normal(key, (CACHE, KV, HD), jnp.float32) * 3.0
    return jnp.clip(drawn, -18.0, 18.0).reshape(CACHE, KV * HD).astype(jnp.bfloat16)


def draw_dec_queries(key, part):
    key = jax.random.fold_in(key, 4)
    drawn = jax.random.normal(key, (STEPS, REQ, HQ, HD), jnp.float32)
    return jnp.clip(drawn, -16.0, 16.0).reshape(STEPS, REQ, HQ * HD).astype(jnp.bfloat16)


def draw_cache_lengths(key, part):
    key = jax.random.fold_in(key, 7)
    first_key, second_key, third_key = jax.random.split(key, 3)
    lengths = jax.random.randint(first_key, (REQ,), CACHE // 8, CACHE + 1)
    longest = jax.random.randint(second_key, (), 0, REQ)
    shortest = (longest + 1 + jax.random.randint(third_key, (), 0, REQ - 1)) % REQ
    lengths = lengths.at[longest].set(CACHE).at[shortest].set(CACHE // 8)
    return lengths.astype(jnp.int32)


def levels(key, dims, pieces, least, largest):
    gain, own = 1.0, jax.random.fold_in(key, 6)
    for dim, shards_of in pieces:
        draws = jnp.exp(jax.random.uniform(jax.random.fold_in(own, dim), (shards_of,), jnp.float32, least / len(pieces), largest / len(pieces)))
        gain = gain * jnp.repeat(draws, dims[dim] // shards_of).reshape([-1 if axis == dim else 1 for axis in range(len(dims))])
    return gain


def bell_draw(key, extent, scale, limit, pieces=(), kind=jnp.bfloat16):
    factor_of = levels(key, extent, pieces, -0.22, 0.18) if pieces else 1.0
    values = jax.random.normal(key, extent, jnp.float32) * scale * factor_of
    return jnp.minimum(jnp.maximum(values, -limit), limit).astype(kind)


def setup_inputs(seed: int = 0) -> dict:
    seeds = jax.random.split(jax.random.key(seed), 13)
    return {
        "ctx_queries": draw_ctx_queries(jax.random.fold_in(seeds[12], 71), 0),
        "ctx_keys": draw_ctx_keys(jax.random.fold_in(seeds[12], 71), 0),
        "ctx_values": bell_draw(seeds[2], (CTXTOK, KV * HD), 1.0, 6.0, ((0, 64), (1, 4))),
        "block_map": jax.random.permutation(seeds[3], N_CTX).astype(jnp.int32),
        "cache_keys": draw_cache_keys(jax.random.fold_in(seeds[12], 71), 0),
        "cache_values": bell_draw(seeds[5], (CACHE, KV * HD), 1.0, 6.0, ((0, 64), (1, 4))),
        "dec_queries": draw_dec_queries(jax.random.fold_in(seeds[12], 71), 0),
        "new_keys": bell_draw(seeds[7], (STEPS, REQ, KV * HD), 3.0, 15.0, ((1, 64), (2, 4))),
        "new_values": bell_draw(seeds[8], (STEPS, REQ, KV * HD), 1.0, 6.0, ((1, 64), (2, 4))),
        "cache_lengths": draw_cache_lengths(jax.random.fold_in(seeds[12], 71), 0),
        "owner": jax.random.permutation(seeds[10], REQ).astype(jnp.int32),
        "out_weight": bell_draw(seeds[11], (HQ * HD, D), (HQ * HD) ** -0.5, 0.0625, ((0, 4), (1, 64))),
    }


LOW_SCORE = -1e+30

def rounded(values):
    return lax.optimization_barrier(values.astype(jnp.bfloat16)).astype(jnp.float32)

def combine(first, second):
    highest = jnp.maximum(first[0], second[0])
    first_factor = jnp.exp(first[0] - highest)
    second_factor = jnp.exp(second[0] - highest)
    return (highest, first[1] * first_factor + second[1] * second_factor, first[2] * first_factor[..., None] + second[2] * second_factor[..., None])

def reference(ctx_queries, ctx_keys, ctx_values, block_map, cache_keys, cache_values, dec_queries, new_keys, new_values, cache_lengths, owner, out_weight):
    group_size = HQ // KV
    score_scale = 1.0 / math.sqrt(HD)
    anchor_index = jnp.sum(jnp.where(block_map == 0, jnp.arange(N_CTX, dtype=jnp.int32), 0)).astype(jnp.int32)
    anchor_keys = lax.dynamic_slice_in_dim(ctx_keys, anchor_index * BLK, BLK, 0).reshape(BLK, KV, HD).astype(jnp.float32)
    anchor_values = lax.dynamic_slice_in_dim(ctx_values, anchor_index * BLK, BLK, 0).reshape(BLK, KV, HD).astype(jnp.float32)
    causal = jnp.arange(BLK)[:, None] >= jnp.arange(BLK)[None, :]

    def one_block(block_index):
        first_row = block_index * BLK
        queries = lax.dynamic_slice_in_dim(ctx_queries, first_row, BLK, 0).reshape(BLK, KV, group_size, HD).astype(jnp.float32)
        own_keys = lax.dynamic_slice_in_dim(ctx_keys, first_row, BLK, 0).reshape(BLK, KV, HD).astype(jnp.float32)
        own_values = lax.dynamic_slice_in_dim(ctx_values, first_row, BLK, 0).reshape(BLK, KV, HD).astype(jnp.float32)
        is_first = block_map[block_index] == 0
        own_scores = jnp.einsum('tkgd,skd->kgts', queries, own_keys) * score_scale
        own_scores = jnp.where(causal, own_scores, LOW_SCORE)
        anchor_scores = jnp.einsum('tkgd,skd->kgts', queries, anchor_keys) * score_scale
        anchor_scores = jnp.where(is_first, LOW_SCORE, anchor_scores)
        highest = jnp.maximum(lax.optimization_barrier(jnp.max(own_scores, -1)), lax.optimization_barrier(jnp.max(anchor_scores, -1)))
        own_weights = jnp.exp(own_scores - highest[..., None])
        anchor_weights = jnp.exp(anchor_scores - highest[..., None])
        row_total = lax.optimization_barrier(jnp.sum(own_weights, -1)) + lax.optimization_barrier(jnp.sum(anchor_weights, -1))
        weighted = jnp.einsum('kgts,skd->kgtd', rounded(own_weights), own_values)
        weighted = weighted + jnp.einsum('kgts,skd->kgtd', rounded(anchor_weights), anchor_values)
        result = weighted / row_total[..., None]
        return jnp.transpose(result, (2, 0, 1, 3)).reshape(BLK, HQ * HD).astype(jnp.bfloat16)
    ctx_out = lax.map(one_block, jnp.arange(N_CTX, dtype=jnp.int32)).reshape(CTXTOK, HQ * HD)
    slot_lengths = jnp.zeros((REQ,), jnp.int32).at[owner].set(cache_lengths)
    step_queries = dec_queries.reshape(STEPS, REQ, KV, group_size, HD).astype(jnp.float32)

    def shard_step(carried, shard_index):
        first_row = shard_index * CACHE_DEV
        shard_keys = lax.dynamic_slice_in_dim(cache_keys, first_row, CACHE_DEV, 0).reshape(CACHE_DEV, KV, HD).astype(jnp.float32)
        shard_values = lax.dynamic_slice_in_dim(cache_values, first_row, CACHE_DEV, 0).reshape(CACHE_DEV, KV, HD).astype(jnp.float32)
        positions = first_row + jnp.arange(CACHE_DEV, dtype=jnp.int32)
        valid = (positions[None, :] < slot_lengths[:, None])[None, :, None, None, :]
        scores = jnp.einsum('jpkgd,ckd->jpkgc', step_queries, shard_keys) * score_scale
        scores = jnp.where(valid, scores, LOW_SCORE)
        shard_top = lax.optimization_barrier(jnp.max(scores, -1))
        weights = jnp.where(valid, jnp.exp(scores - shard_top[..., None]), 0.0)
        shard_total = lax.optimization_barrier(jnp.sum(weights, -1))
        shard_sum = jnp.einsum('jpkgc,ckd->jpkgd', rounded(weights), shard_values)
        return (combine(carried, (shard_top, shard_total, shard_sum)), None)
    start_state = (jnp.full((STEPS, REQ, KV, group_size), LOW_SCORE, jnp.float32), jnp.zeros((STEPS, REQ, KV, group_size), jnp.float32), jnp.zeros((STEPS, REQ, KV, group_size, HD), jnp.float32))
    merged, unused = lax.scan(shard_step, start_state, jnp.arange(N_CTX, dtype=jnp.int32))
    recent_keys = new_keys.reshape(STEPS, REQ, KV, HD).astype(jnp.float32)
    recent_values = new_values.reshape(STEPS, REQ, KV, HD).astype(jnp.float32)
    earlier = (jnp.arange(STEPS)[None, :] <= jnp.arange(STEPS)[:, None])[:, None, None, None, :]
    recent_scores = jnp.einsum('jpkgd,ipkd->jpkgi', step_queries, recent_keys) * score_scale
    recent_scores = jnp.where(earlier, recent_scores, LOW_SCORE)
    recent_top = lax.optimization_barrier(jnp.max(recent_scores, -1))
    recent_weights = jnp.where(earlier, jnp.exp(recent_scores - recent_top[..., None]), 0.0)
    recent_total = lax.optimization_barrier(jnp.sum(recent_weights, -1))
    recent_sum = jnp.einsum('jpkgi,ipkd->jpkgd', rounded(recent_weights), recent_values)
    final = combine(merged, (recent_top, recent_total, recent_sum))
    attention = (final[2] / final[1][..., None]).reshape(STEPS, REQ, HQ * HD).astype(jnp.bfloat16)
    ordered = attention[:, owner]
    projected = jnp.dot(ordered.reshape(STEPS * REQ, HQ * HD), out_weight, preferred_element_type=jnp.float32)
    dec_out = projected.reshape(STEPS, REQ, D).astype(jnp.bfloat16)
    return (ctx_out, dec_out)
```

```python
import functools
import math

import jax
import jax.numpy as jnp
from jax import lax
from jax.experimental import pallas as pl
from jax.experimental.pallas import tpu as pltpu
from jax.sharding import Mesh, PartitionSpec as P

HD = 128
STEPS = 4
NZ, NY, NC, NX = 8, 4, 2, 4
ROWS = 256
SLOTS = 64
SCALE2 = math.log2(math.e) / math.sqrt(HD)
LOW = -1e29
FLOOR = -1e28
F32 = jnp.float32
BF16 = jnp.bfloat16
VMEM = pl.BlockSpec(memory_space=pltpu.VMEM)
SMEM = pl.BlockSpec(memory_space=pltpu.SMEM)
NT = (((1,), (1,)), ((), ()))
NN = (((1,), (0,)), ((), ()))


def iota(shape, dim):
    return lax.broadcasted_iota(jnp.int32, shape, dim)


def dot(a, b, dims=NN):
    return lax.dot_general(a, b, dims, preferred_element_type=F32)


def params(mib=20):
    return pltpu.CompilerParams(vmem_limit_bytes=mib * 2**20)


def cost(flops, moved, trans=0):
    return pl.CostEstimate(flops=flops, bytes_accessed=moved, transcendentals=trans)


def prep_kernel(dq, nk, nv, ck, cv, xk, xv, q_out, p0, p1, p2, p3, scratch, dq_v, nk_v, nv_v, xk_v, xv_v, sems):
    y = lax.axis_index("y")
    copies = [
        (dq, dq_v),
        (nk, nk_v),
        (nv, nv_v),
        (ck, p0.at[0:ROWS, :]),
        (cv, p0.at[ROWS : 2 * ROWS, :]),
        (xk, xk_v),
        (xv, xv_v),
    ]
    copies = [pltpu.make_async_copy(src, dst, sems.at[i]) for i, (src, dst) in enumerate(copies)]
    for copy in copies:
        copy.start()
    scratch[...] = jnp.zeros_like(scratch)
    row, col = iota((80, 160), 0), iota((80, 160), 1)
    pick = (col == (row // 4) * 8 + row % 4).astype(F32).astype(BF16)
    for copy in copies[:3]:
        copy.wait()
    for h in range(16):
        scratch[h * 8 : h * 8 + 4, :] = dq_v[:, h * HD : (h + 1) * HD].astype(F32)
    for i, ref in enumerate((nk_v, nv_v)):
        for k in range(2):
            at = 128 + (i * 2 + k) * 8
            scratch[at : at + 4, :] = ref[:, k * HD : (k + 1) * HD].astype(F32)
    packed = dot(pick, scratch[...].astype(BF16)).astype(BF16)
    for s in range(NZ):
        q_out[s] = packed
    for copy in copies[3:]:
        copy.wait()
    shard = p0[0 : 2 * ROWS, :]
    for out in (p1, p2, p3):
        out[0 : 2 * ROWS, :] = shard
    for s, out in enumerate((p0, p1, p2, p3)):
        for i in range(8):
            source, k = (xk_v, xv_v)[i // 4], (i % 4) // 2
            for core in range(2):
                at = lax.rem(y + s, NY) * 64 + core * 32 + (i % 2) * 16
                tile = source[pl.ds(pl.multiple_of(at, 16), 16), k * HD : (k + 1) * HD]
                out[512 + i * 16 : 528 + i * 16, core * HD : (core + 1) * HD] = tile


def prep(*args):
    args = [pltpu.with_memory_space_constraint(a, pltpu.HBM) for a in args]
    payload = jax.ShapeDtypeStruct((640, 256), BF16)
    return pl.pallas_call(
        prep_kernel,
        out_shape=(jax.ShapeDtypeStruct((NZ, 80, HD), BF16),) + (payload,) * 4,
        in_specs=[pl.BlockSpec(memory_space=pltpu.HBM)] * 7,
        out_specs=(VMEM,) * 5,
        scratch_shapes=[
            pltpu.VMEM((160, HD), F32),
            pltpu.VMEM((STEPS, 2048), BF16),
            pltpu.VMEM((STEPS, 256), BF16),
            pltpu.VMEM((STEPS, 256), BF16),
            pltpu.VMEM((ROWS, 256), BF16),
            pltpu.VMEM((ROWS, 256), BF16),
            pltpu.SemaphoreType.DMA((7,)),
        ],
        compiler_params=params(),
        cost_estimate=cost(1 << 20, 1 << 20),
        name="prep",
    )(*args)


def line_kernel(g, owner, lengths, blocks, q_out, ro_out, rm_out, rl_out, meta):
    z, y, c = lax.axis_index("z"), lax.axis_index("y"), lax.axis_index("c")
    line = y * NC + c
    for s in range(8):
        meta[s] = 0

    def scan_slots(r, root):
        slot = owner[r]

        @pl.when(lax.rem(slot, 8) == line)
        def _():
            meta[slot // 8] = lengths[r]

        return jnp.where(blocks[r] == 0, r, root)

    root = lax.fori_loop(0, SLOTS, scan_slots, jnp.int32(0))
    meta[8] = root // 8
    meta[9] = lax.rem(root, 8) // 2
    meta[10] = lax.rem(root, 2)

    row, col = iota((256, 256), 0), iota((256, 256), 1)
    source = lax.rem(row // 4, 8) * 32 + (row // 32) * 4 + lax.rem(row, 4)
    pick = (col == source).astype(F32).astype(BF16)
    for k in range(2):
        natural = jnp.concatenate([g[s, k * 32 : (k + 1) * 32, :] for s in range(NZ)], axis=0)
        q_out[k * 256 : (k + 1) * 256, :] = dot(pick, natural).astype(BF16)
    mine = q_out[pl.ds(pl.multiple_of(z * 64, 64), 64), :]
    tokens = jnp.concatenate([g[s, 64:80, :] for s in range(NZ)], axis=0)
    wide = tokens.astype(F32)
    values = jnp.concatenate([wide[8:], wide[:8]], axis=0).astype(BF16)
    scores = dot(mine, tokens, NT) * SCALE2
    row, col = iota((64, 128), 0), iota((64, 128), 1)
    seen = (
        (lax.rem(row // 4, 8) == col // 16)
        & (lax.rem(col, 16) // 4 == z // 4)
        & (lax.rem(col, 4) <= lax.rem(row, 4))
    )
    scores = jnp.where(seen, scores, LOW)
    top = jnp.max(scores, axis=1, keepdims=True)
    weights = jnp.exp2(scores - top)
    rm_out[...] = jnp.broadcast_to(top, (64, HD))
    rl_out[...] = jnp.broadcast_to(jnp.sum(weights, axis=1, keepdims=True), (64, HD))
    ro_out[...] = dot(weights.astype(BF16), values)


def line_part(gathered, owner, lengths, blocks):
    part = jax.ShapeDtypeStruct((64, HD), F32)
    return pl.pallas_call(
        line_kernel,
        out_shape=(
            jax.ShapeDtypeStruct((512, HD), BF16),
            part,
            part,
            part,
            jax.ShapeDtypeStruct((16,), jnp.int32),
        ),
        in_specs=[VMEM, SMEM, SMEM, SMEM],
        out_specs=(VMEM, VMEM, VMEM, VMEM, SMEM),
        compiler_params=params(),
        cost_estimate=cost(1 << 24, 1 << 20),
        name="line_part",
    )(gathered, owner, lengths, blocks)


def shard_kernel(meta, q, *refs):
    bufs, out, scores = refs[:8], refs[8], refs[9]
    z, y, c = lax.axis_index("z"), lax.axis_index("y"), lax.axis_index("c")
    rowslot = iota((32, HD), 0) // 4
    length = jnp.zeros((32, HD), jnp.int32)
    for s in range(8):
        length = jnp.where(rowslot == s, meta[s], length)
    lane = iota((32, HD), 1)
    for k in range(2):
        qk = q[k * 256 : (k + 1) * 256, :]
        tops = []
        for b in range(8):
            shift, swap = b % 4, b // 4
            shard = z * 8 + lax.rem(y - shift + NY, NY) * NC + (c if swap == 0 else 1 - c)
            room = length - shard * ROWS
            keep = jnp.concatenate([lane < room, lane + HD < room], axis=1)
            raw = dot(qk, bufs[b][0:ROWS, k * HD : (k + 1) * HD], NT)
            raw = jnp.where(keep[None], raw.reshape(8, 32, 256), LOW).reshape(256, 256)
            scores[b] = raw
            tops.append(
                jnp.max(jnp.maximum(raw[:, :HD], raw[:, HD:]), axis=1, keepdims=True)
            )
        top = functools.reduce(jnp.maximum, tops) * SCALE2
        top = top.astype(BF16).astype(F32)
        total = jnp.zeros((256, HD), F32)
        weighted = jnp.zeros((256, HD), F32)
        for b in range(8):
            weights = jnp.exp2((scores[b] - jnp.maximum(tops[b], FLOOR)) * SCALE2)
            factor = jnp.exp2(jnp.minimum(tops[b] * SCALE2 - top, 64.0))
            total = total + (weights[:, :HD] + weights[:, HD:]) * factor
            weighted = weighted + factor * dot(
                weights.astype(BF16), bufs[b][ROWS : 2 * ROWS, k * HD : (k + 1) * HD]
            )
        total = jnp.sum(total, axis=1, keepdims=True)
        total_high = total.astype(BF16).astype(F32)
        total_low = total - total_high
        column = iota((256, HD), 1)
        stats = jnp.where(
            column == 0, top, jnp.where(column == 1, total_high, jnp.where(column == 2, total_low, 0.0))
        )
        weighted = weighted.astype(BF16)
        for pair in range(2):
            flipped = jnp.transpose(stats[pair * 128 : (pair + 1) * 128])[:16].astype(BF16)
            out[k * 4 + pair * 2, 64:80, :] = flipped
            out[k * 4 + pair * 2 + 1, 64:80, :] = flipped
        for part in range(4):
            out[k * 4 + part, 0:64, :] = weighted[part * 64 : (part + 1) * 64]
    root_shift = lax.rem(y - meta[9] + NY, NY)
    root_swap = jnp.where(meta[10] == c, 0, 1)
    for b in range(8):
        for core in range(2):

            @pl.when((root_shift == b % 4) & (root_swap == b // 4) & (c == core))
            def _(b=b, core=core):
                for piece in range(NZ):
                    out[piece, 80:96, :] = bufs[b][
                        512 + piece * 16 : 528 + piece * 16, core * HD : (core + 1) * HD
                    ]


def shard_part(meta, q, bufs):
    return pl.pallas_call(
        shard_kernel,
        out_shape=jax.ShapeDtypeStruct((NZ, 96, HD), BF16),
        in_specs=[SMEM] + [VMEM] * 9,
        out_specs=VMEM,
        scratch_shapes=[pltpu.VMEM((8, 256, 256), F32)],
        compiler_params=params(),
        cost_estimate=cost(1 << 30, 4 << 20, 1 << 20),
        name="shard_part",
    )(meta, q, *bufs)


def merge_kernel(meta, parts, ro, rm, rl, out, scratch):
    z = lax.axis_index("z")
    stats = jnp.concatenate([parts[j, 64:80, :] for j in range(NZ)], axis=0).astype(F32)
    scratch[...] = jnp.transpose(stats)
    mine = scratch[pl.ds(pl.multiple_of(lax.rem(z, 2) * 64, 64), 64), :]
    tops = [mine[:, j * 16 : j * 16 + 1] for j in range(NZ)]
    totals = [mine[:, j * 16 + 1 : j * 16 + 2] + mine[:, j * 16 + 2 : j * 16 + 3] for j in range(NZ)]
    top = rm[...]
    for t in tops:
        top = jnp.maximum(top, t)
    factor = jnp.exp2(rm[...] - top)
    total = rl[...] * factor
    weighted = ro[...] * factor
    for j in range(NZ):
        factor = jnp.exp2(tops[j] - top)
        total = total + totals[j] * factor
        weighted = weighted + parts[j, 0:64, :].astype(F32) * factor
    attention = (weighted / total).astype(BF16)
    anchor = parts[meta[8], 80:96, :]
    for s in range(NZ):
        out[s, 0:64, :] = attention
        out[s, 64:80, :] = anchor


def merge(meta, parts, ro, rm, rl):
    return pl.pallas_call(
        merge_kernel,
        out_shape=jax.ShapeDtypeStruct((NZ, 80, HD), BF16),
        in_specs=[SMEM] + [VMEM] * 4,
        out_specs=VMEM,
        scratch_shapes=[pltpu.VMEM((HD, HD), F32)],
        compiler_params=params(),
        cost_estimate=cost(1 << 20, 1 << 19),
        name="merge",
    )(meta, parts, ro, rm, rl)


def project_kernel(owner, w, *refs):
    bufs, outs = refs[:8], refs[8:12]
    y, c, x = lax.axis_index("y"), lax.axis_index("c"), lax.axis_index("x")
    total = jnp.zeros((256, HD), F32)
    for zz in range(NZ):
        left = jnp.concatenate([b[zz, 0:32, :] for b in bufs], axis=0)
        right = jnp.concatenate([b[zz, 32:64, :] for b in bufs], axis=0)
        total = total + dot(
            jnp.concatenate([left, right], axis=1), w[zz * 256 : (zz + 1) * 256, :]
        )
    high = total.astype(BF16)
    low = (total - high.astype(F32)).astype(BF16)
    col = iota((64, 256), 1)
    buf = col // 32
    slot = (
        lax.rem(col // 4, 8) * 8
        + lax.rem(y - lax.rem(buf, 4) + NY, NY) * NC
        + jnp.where(buf >= 4, 1 - c, c)
    )
    row = iota((64, 256), 0)
    same_step = lax.rem(col, 4) == row // 16
    request = lax.rem(row, 16)
    for s, out in enumerate(outs):
        first = lax.rem(x + s, NX) * 16
        wanted = jnp.zeros((64, 256), jnp.int32)
        for j in range(16):
            wanted = jnp.where(request == j, owner[first + j], wanted)
        pick = ((wanted == slot) & same_step).astype(F32).astype(BF16)
        out[...] = dot(pick, high) + dot(pick, low)


def project(owner, w, bufs):
    return pl.pallas_call(
        project_kernel,
        out_shape=(jax.ShapeDtypeStruct((64, HD), F32),) * 4,
        in_specs=[SMEM] + [VMEM] * 9,
        out_specs=(VMEM,) * 4,
        compiler_params=params(),
        cost_estimate=cost(1 << 28, 2 << 20),
        name="project",
    )(owner, w, *bufs)


def own_kernel(q, xk, xv, out, lse, values):
    for k in range(2):
        values[k, :, 0:HD] = xv[:, k * HD : (k + 1) * HD]
        values[k, :, HD:] = jnp.ones((ROWS, HD), BF16)
    causal = iota((128, 128), 0) >= iota((128, 128), 1)
    for group in range(4):
        units = [(group * 4 + h, half) for h in range(4) for half in range(2)]
        tiles, tops = [], []
        for h, half in units:
            near = (half + 1) * 128
            keys = xk[0:near, (h // 8) * HD : (h // 8 + 1) * HD]
            own = dot(q[near - 128 : near, h * HD : (h + 1) * HD], keys, NT)
            diagonal = jnp.where(causal, own[:, near - 128 :], LOW)
            tiles.append([own[:, :HD], diagonal] if half else [diagonal])
        for parts in tiles:
            tops.append(
                jnp.max(functools.reduce(jnp.maximum, parts), axis=1, keepdims=True) * SCALE2
            )
        for (h, half), parts, top in zip(units, tiles, tops):
            near = (half + 1) * 128
            weights = [jnp.exp2(t * SCALE2 - top).astype(BF16) for t in parts]
            weights = jnp.concatenate(weights, axis=1) if half else weights[0]
            summed = dot(weights, values[h // 8, 0:near, :])
            rows, lanes = slice(near - 128, near), slice(h * HD, (h + 1) * HD)
            out[rows, lanes] = summed[:, :HD] / summed[:, HD:]
            lse[rows, lanes] = top + jnp.log2(summed[:, HD:])


def context_own(q, xk, xv):
    whole = jax.ShapeDtypeStruct((ROWS, 2048), F32)
    return pl.pallas_call(
        own_kernel,
        out_shape=(whole, whole),
        in_specs=[VMEM] * 3,
        out_specs=(VMEM, VMEM),
        scratch_shapes=[pltpu.VMEM((2, ROWS, 2 * HD), BF16)],
        compiler_params=params(),
        cost_estimate=cost(1 << 30, 6 << 20, 1 << 20),
        name="context_own",
    )(q, xk, xv)


def far_kernel(blocks, q, own, lse, *refs):
    bufs, (out, keys, values, staged, sems) = refs[:8], refs[8:]
    index = (lax.axis_index("z") * NY + lax.axis_index("y")) * NC + lax.axis_index("c")
    hide = jnp.where(blocks[index] == 0, LOW, 0.0).astype(F32)
    for k in range(2):
        values[k, :, HD:] = jnp.ones((ROWS, HD), BF16)
        for j, buf in enumerate(bufs):
            for half in range(2):
                at, tile = j * 32 + half * 16, k * 2 + half
                keys[k, at : at + 16, :] = buf[tile, 64:80, :]
                values[k, at : at + 16, 0:HD] = buf[4 + tile, 64:80, :]
    copies = []
    for group in range(4):
        units = [(group * 4 + h, half) for h in range(4) for half in range(2)]
        tiles = []
        for h, half in units:
            queries = q[half * 128 : (half + 1) * 128, h * HD : (h + 1) * HD]
            far = dot(queries, keys[h // 8], NT) + hide
            tiles.append([far[:, :HD], far[:, HD:]])
        tops = [jnp.max(jnp.maximum(*t), axis=1, keepdims=True) * SCALE2 for t in tiles]
        for (h, half), parts, top in zip(units, tiles, tops):
            rows, lanes = slice(half * 128, (half + 1) * 128), slice(h * HD, (h + 1) * HD)
            near = lse[rows, lanes]
            top = jnp.maximum(top, near)
            weights = [jnp.exp2(t * SCALE2 - top).astype(BF16) for t in parts]
            summed = dot(jnp.concatenate(weights, axis=1), values[h // 8])
            factor = jnp.exp2(near - top)
            joint = summed[:, :HD] + factor * own[rows, lanes]
            staged[rows, lanes] = (joint / (summed[:, HD:] + factor)).astype(BF16)
        lanes = slice(group * 512, (group + 1) * 512)
        copies.append(pltpu.make_async_copy(staged.at[:, lanes], out.at[:, lanes], sems.at[group]))
        copies[-1].start()
    for copy in copies:
        copy.wait()


def context_far(blocks, q, own, lse, bufs):
    return pl.pallas_call(
        far_kernel,
        out_shape=jax.ShapeDtypeStruct((ROWS, 2048), BF16),
        in_specs=[SMEM] + [VMEM] * 11,
        out_specs=pl.BlockSpec(memory_space=pl.ANY),
        scratch_shapes=[
            pltpu.VMEM((2, ROWS, HD), BF16),
            pltpu.VMEM((2, ROWS, 2 * HD), BF16),
            pltpu.VMEM((ROWS, 2048), BF16),
            pltpu.SemaphoreType.DMA((4,)),
        ],
        compiler_params=params(),
        cost_estimate=cost(1 << 30, 6 << 20, 1 << 20),
        name="context_far",
    )(blocks, q, own, lse, *bufs)


def shifted(value, axis, size, shift):
    return lax.ppermute(value, axis, [(i, (i + shift) % size) for i in range(size)])


def on_device(
    ctx_queries,
    ctx_keys,
    ctx_values,
    block_map,
    cache_keys,
    cache_values,
    dec_queries,
    new_keys,
    new_values,
    cache_lengths,
    owner,
    out_weight,
):
    packed, *payloads = prep(
        dec_queries.reshape(STEPS, -1),
        new_keys.reshape(STEPS, -1),
        new_values.reshape(STEPS, -1),
        cache_keys,
        cache_values,
        ctx_keys,
        ctx_values,
    )
    shards = [shifted(payloads[s], "y", NY, s) for s in range(1, NY)]
    gathered = lax.all_to_all(packed, "z", 0, 0, tiled=True)
    own, lse = context_own(ctx_queries, ctx_keys, ctx_values)
    gathered, own, lse, *shards = lax.optimization_barrier((gathered, own, lse, *shards))
    shards = [payloads[0]] + shards
    shards = shards + [shifted(b, "c", NC, 1) for b in shards]
    q, ro, rm, rl, meta = line_part(gathered, owner, cache_lengths, block_map)
    parts = lax.all_to_all(shard_part(meta, q, shards), "z", 0, 0, tiled=True)
    merged = lax.all_to_all(merge(meta, parts, ro, rm, rl), "z", 0, 0, tiled=True)
    lines = [merged] + [shifted(merged, "y", NY, s) for s in range(1, NY)]
    everything = lines + [shifted(b, "c", NC, 1) for b in lines]
    ctx_out = context_far(block_map, ctx_queries, own, lse, everything)
    mine, *others = project(owner, out_weight, everything)
    total = mine
    for s, part in enumerate(others):
        total = total + shifted(part, "x", NX, s + 1)
    dec_out = total.astype(BF16).reshape(STEPS, 16, HD)
    return (ctx_out, dec_out)


def solution(mesh):
    grid = Mesh(mesh.devices.reshape(NZ, NY, NC, NX), ("z", "y", "c", "x"))
    ctx = ("z", "y", "c")
    in_specs = (
        P(ctx, "x"),
        P(ctx, "x"),
        P(ctx, "x"),
        P(),
        P(ctx, "x"),
        P(ctx, "x"),
        P(None, ctx, "x"),
        P(None, ctx, "x"),
        P(None, ctx, "x"),
        P(),
        P(),
        P("x", ctx),
    )
    out_specs = (P(ctx, "x"), P(None, "x", ctx))
    return jax.shard_map(on_device, mesh=grid, in_specs=in_specs, out_specs=out_specs, check_vma=False)
```

```python
import functools
import math

import jax
import jax.numpy as jnp
from jax import lax
from jax.experimental import pallas as pl
from jax.experimental.pallas import tpu as pltpu
from jax.sharding import Mesh, PartitionSpec as P

HD = 128
STEPS = 4
NZ, NY, NC, NX = 8, 4, 2, 4
ROWS = 256
SLOTS = 64
SCALE2 = math.log2(math.e) / math.sqrt(HD)
LOW = -1e29
FLOOR = -(2.0**80)
F32 = jnp.float32
BF16 = jnp.bfloat16
VMEM = pl.BlockSpec(memory_space=pltpu.VMEM)
SMEM = pl.BlockSpec(memory_space=pltpu.SMEM)
NT = (((1,), (1,)), ((), ()))
NN = (((1,), (0,)), ((), ()))


def iota(shape, dim):
    return lax.broadcasted_iota(jnp.int32, shape, dim)


def dot(a, b, dims=NN):
    return lax.dot_general(a, b, dims, preferred_element_type=F32)


def params(mib=16):
    return pltpu.CompilerParams(vmem_limit_bytes=mib * 2**20)


def cost(flops, moved, trans=0):
    return pl.CostEstimate(flops=flops, bytes_accessed=moved, transcendentals=trans)


def prep_kernel(dq, nk, nv, ck, cv, xk, xv, q_out, p0, p1, p2, p3, scratch, dq_v, nk_v, nv_v, xk_v, xv_v, sems):
    y = lax.axis_index("y")
    copies = [
        (dq, dq_v),
        (nk, nk_v),
        (nv, nv_v),
        (ck, p0.at[0:ROWS, :]),
        (cv, p0.at[ROWS : 2 * ROWS, :]),
        (xk, xk_v),
        (xv, xv_v),
    ]
    copies = [pltpu.make_async_copy(src, dst, sems.at[i]) for i, (src, dst) in enumerate(copies)]
    for copy in copies:
        copy.start()
    scratch[...] = jnp.zeros_like(scratch)
    row, col = iota((80, 160), 0), iota((80, 160), 1)
    pick = (col == (row // 4) * 8 + row % 4).astype(F32).astype(BF16)
    for copy in copies[:3]:
        copy.wait()
    for h in range(16):
        scratch[h * 8 : h * 8 + 4, :] = dq_v[:, h * HD : (h + 1) * HD].astype(F32)
    for i, ref in enumerate((nk_v, nv_v)):
        for k in range(2):
            at = 128 + (i * 2 + k) * 8
            scratch[at : at + 4, :] = ref[:, k * HD : (k + 1) * HD].astype(F32)
    packed = dot(pick, scratch[...].astype(BF16)).astype(BF16)
    for s in range(NZ):
        q_out[s] = packed
    for copy in copies[3:]:
        copy.wait()
    shard = p0[0 : 2 * ROWS, :]
    for out in (p1, p2, p3):
        out[0 : 2 * ROWS, :] = shard
    for s, out in enumerate((p0, p1, p2, p3)):
        for i in range(8):
            source, k = (xk_v, xv_v)[i // 4], (i % 4) // 2
            for core in range(2):
                at = lax.rem(y + s, NY) * 64 + core * 32 + (i % 2) * 16
                tile = source[pl.ds(pl.multiple_of(at, 16), 16), k * HD : (k + 1) * HD]
                out[512 + i * 16 : 528 + i * 16, core * HD : (core + 1) * HD] = tile


def prep(*args):
    args = [pltpu.with_memory_space_constraint(a, pltpu.HBM) for a in args]
    payload = jax.ShapeDtypeStruct((640, 256), BF16)
    return pl.pallas_call(
        prep_kernel,
        out_shape=(jax.ShapeDtypeStruct((NZ, 80, HD), BF16),) + (payload,) * 4,
        in_specs=[pl.BlockSpec(memory_space=pltpu.HBM)] * 7,
        out_specs=(VMEM,) * 5,
        scratch_shapes=[
            pltpu.VMEM((160, HD), F32),
            pltpu.VMEM((STEPS, 2048), BF16),
            pltpu.VMEM((STEPS, 256), BF16),
            pltpu.VMEM((STEPS, 256), BF16),
            pltpu.VMEM((ROWS, 256), BF16),
            pltpu.VMEM((ROWS, 256), BF16),
            pltpu.SemaphoreType.DMA((7,)),
        ],
        compiler_params=params(),
        cost_estimate=cost(1 << 20, 1 << 20),
        name="prep",
    )(*args)


def line_kernel(g, q_out, ro_out, rm_out, rl_out):
    z = lax.axis_index("z")
    row, col = iota((256, 256), 0), iota((256, 256), 1)
    source = lax.rem(row // 4, 8) * 32 + (row // 32) * 4 + lax.rem(row, 4)
    pick = (col == source).astype(F32).astype(BF16)
    for k in range(2):
        natural = jnp.concatenate([g[s, k * 32 : (k + 1) * 32, :] for s in range(NZ)], axis=0)
        q_out[k * 256 : (k + 1) * 256, :] = dot(pick, natural).astype(BF16)
    mine = q_out[pl.ds(pl.multiple_of(z * 64, 64), 64), :]
    tokens = jnp.concatenate([g[s, 64:80, :] for s in range(NZ)], axis=0)
    wide = tokens.astype(F32)
    values = jnp.concatenate([wide[8:], wide[:8]], axis=0).astype(BF16)
    scores = dot(mine, tokens, NT) * SCALE2
    row, col = iota((64, 128), 0), iota((64, 128), 1)
    seen = (
        (lax.rem(row // 4, 8) == col // 16)
        & (lax.rem(col, 16) // 4 == z // 4)
        & (lax.rem(col, 4) <= lax.rem(row, 4))
    )
    scores = jnp.where(seen, scores, LOW)
    top = jnp.max(scores, axis=1, keepdims=True)
    weights = jnp.exp2(scores - top)
    rm_out[...] = jnp.broadcast_to(top, (64, HD))
    rl_out[...] = jnp.broadcast_to(jnp.sum(weights, axis=1, keepdims=True), (64, HD))
    ro_out[...] = dot(weights.astype(BF16), values)


def line_part(gathered):
    part = jax.ShapeDtypeStruct((64, HD), F32)
    return pl.pallas_call(
        line_kernel,
        out_shape=(jax.ShapeDtypeStruct((512, HD), BF16), part, part, part),
        in_specs=[VMEM],
        out_specs=(VMEM,) * 4,
        compiler_params=params(),
        cost_estimate=cost(1 << 24, 1 << 20),
        name="line_part",
    )(gathered)


def shard_scores(meta, q, bufs, k, core, scores):
    z, y = lax.axis_index("z"), lax.axis_index("y")
    rowslot = iota((32, HD), 0) // 4
    length = jnp.zeros((32, HD), jnp.int32)
    for s in range(8):
        length = jnp.where(rowslot == s, meta[s], length)
    lane = iota((32, HD), 1)
    tops = []
    for b in range(4):
        room = length - (z * 8 + lax.rem(y - b + NY, NY) * NC + core) * ROWS
        keep = jnp.concatenate([lane < room, lane + HD < room], axis=1)
        raw = dot(q[k * 256 : (k + 1) * 256, :], bufs[b][0:ROWS, k * HD : (k + 1) * HD], NT)
        raw = jnp.where(keep[None], raw.reshape(8, 32, 256), LOW).reshape(256, 256)
        scores[k, b] = raw
        tops.append(jnp.max(jnp.maximum(raw[:, :HD], raw[:, HD:]), axis=1, keepdims=True))
    return tops


def shard_sums(bufs, k, tops, top, scores, total, weighted):
    for b in range(4):
        weights = jnp.exp2((scores[k, b] - tops[b]) * SCALE2)
        factor = jnp.exp2(tops[b] * SCALE2 - top)
        total = total + (weights[:, :HD] + weights[:, HD:]) * factor
        weighted = weighted + factor * dot(
            weights.astype(BF16), bufs[b][ROWS : 2 * ROWS, k * HD : (k + 1) * HD]
        )
    return total, weighted


def first_kernel(meta, q, *refs):
    bufs, (o_out, m_out, l_out, scores) = refs[:4], refs[4:]
    core = lax.axis_index("c")
    tops = [shard_scores(meta, q, bufs, k, core, scores) for k in range(2)]
    zeros = jnp.zeros((256, HD), F32)
    for k in range(2):
        rows = slice(k * 256, (k + 1) * 256)
        top = jnp.maximum(functools.reduce(jnp.maximum, tops[k]) * SCALE2, FLOOR)
        l_out[rows, :], o_out[rows, :] = shard_sums(bufs, k, tops[k], top, scores, zeros, zeros)
        m_out[rows, :] = jnp.broadcast_to(top, (256, HD))


def first_part(meta, q, bufs):
    part = jax.ShapeDtypeStruct((512, HD), F32)
    return pl.pallas_call(
        first_kernel,
        out_shape=(part,) * 3,
        in_specs=[SMEM] + [VMEM] * 5,
        out_specs=(VMEM,) * 3,
        scratch_shapes=[pltpu.VMEM((2, 4, 256, 256), F32)],
        compiler_params=params(),
        cost_estimate=cost(1 << 29, 2 << 20, 1 << 19),
        name="first_part",
    )(meta, q, *bufs)


def second_kernel(meta, q, o, m, l, *refs):
    all_bufs, bufs, (out, scores) = refs[:8], refs[4:8], refs[8:]
    core = 1 - lax.axis_index("c")
    tops = [shard_scores(meta, q, bufs, k, core, scores) for k in range(2)]
    column = iota((256, HD), 1)
    for k in range(2):
        rows = slice(k * 256, (k + 1) * 256)
        top = jnp.maximum(functools.reduce(jnp.maximum, tops[k]) * SCALE2, m[rows, :])
        top = top.astype(BF16).astype(F32)
        factor = jnp.exp2(m[rows, :] - top)
        total, weighted = shard_sums(
            bufs, k, tops[k], top, scores, l[rows, :] * factor, o[rows, :] * factor
        )
        total = jnp.sum(total, axis=1, keepdims=True)
        total_high = total.astype(BF16).astype(F32)
        total_low = total - total_high
        stats = jnp.where(
            column == 0, top, jnp.where(column == 1, total_high, jnp.where(column == 2, total_low, 0.0))
        )
        weighted = weighted.astype(BF16)
        for pair in range(2):
            flipped = jnp.transpose(stats[pair * 128 : (pair + 1) * 128])[:16].astype(BF16)
            out[k * 4 + pair * 2, 64:80, :] = flipped
            out[k * 4 + pair * 2 + 1, 64:80, :] = flipped
        for part in range(4):
            out[k * 4 + part, 0:64, :] = weighted[part * 64 : (part + 1) * 64]
    y, c = lax.axis_index("y"), lax.axis_index("c")
    root_shift = lax.rem(y - meta[9] + NY, NY)
    for b in range(8):
        for lane_half in range(2):
            swapped = b // 4
            from_core = jnp.where(meta[10] == c, 0, 1)

            @pl.when((root_shift == b % 4) & (from_core == swapped) & (c == lane_half))
            def _(b=b, lane_half=lane_half):
                lanes = slice(lane_half * HD, (lane_half + 1) * HD)
                for piece in range(NZ):
                    out[piece, 80:96, :] = all_bufs[b][512 + piece * 16 : 528 + piece * 16, lanes]


def second_part(meta, q, state, bufs):
    return pl.pallas_call(
        second_kernel,
        out_shape=jax.ShapeDtypeStruct((NZ, 96, HD), BF16),
        in_specs=[SMEM] + [VMEM] * 12,
        out_specs=VMEM,
        scratch_shapes=[pltpu.VMEM((2, 4, 256, 256), F32)],
        compiler_params=params(),
        cost_estimate=cost(1 << 29, 2 << 20, 1 << 19),
        name="second_part",
    )(meta, q, *state, *bufs)


def merge_kernel(meta, parts, ro, rm, rl, out, scratch):
    z = lax.axis_index("z")
    stats = jnp.concatenate([parts[j, 64:80, :] for j in range(NZ)], axis=0).astype(F32)
    scratch[...] = jnp.transpose(stats)
    mine = scratch[pl.ds(pl.multiple_of(lax.rem(z, 2) * 64, 64), 64), :]
    tops = [mine[:, j * 16 : j * 16 + 1] for j in range(NZ)]
    totals = [mine[:, j * 16 + 1 : j * 16 + 2] + mine[:, j * 16 + 2 : j * 16 + 3] for j in range(NZ)]
    top = rm[...]
    for t in tops:
        top = jnp.maximum(top, t)
    factor = jnp.exp2(rm[...] - top)
    total = rl[...] * factor
    weighted = ro[...] * factor
    for j in range(NZ):
        factor = jnp.exp2(tops[j] - top)
        total = total + totals[j] * factor
        weighted = weighted + parts[j, 0:64, :].astype(F32) * factor
    attention = (weighted / total).astype(BF16)
    anchor = parts[meta[8], 80:96, :]
    for s in range(NZ):
        out[s, 0:64, :] = attention
        out[s, 64:80, :] = anchor


def merge(meta, parts, ro, rm, rl):
    return pl.pallas_call(
        merge_kernel,
        out_shape=jax.ShapeDtypeStruct((NZ, 80, HD), BF16),
        in_specs=[SMEM] + [VMEM] * 4,
        out_specs=VMEM,
        scratch_shapes=[pltpu.VMEM((HD, HD), F32)],
        compiler_params=params(),
        cost_estimate=cost(1 << 20, 1 << 19),
        name="merge",
    )(meta, parts, ro, rm, rl)


def project_kernel(owner, w, *refs):
    bufs, outs = refs[:8], refs[8:12]
    y, c, x = lax.axis_index("y"), lax.axis_index("c"), lax.axis_index("x")
    total = jnp.zeros((256, HD), F32)
    for zz in range(NZ):
        left = jnp.concatenate([b[zz, 0:32, :] for b in bufs], axis=0)
        right = jnp.concatenate([b[zz, 32:64, :] for b in bufs], axis=0)
        total = total + dot(
            jnp.concatenate([left, right], axis=1), w[zz * 256 : (zz + 1) * 256, :]
        )
    high = total.astype(BF16)
    low = (total - high.astype(F32)).astype(BF16)
    col = iota((64, 256), 1)
    buf = col // 32
    slot = (
        lax.rem(col // 4, 8) * 8
        + lax.rem(y - lax.rem(buf, 4) + NY, NY) * NC
        + jnp.where(buf >= 4, 1 - c, c)
    )
    row = iota((64, 256), 0)
    same_step = lax.rem(col, 4) == row // 16
    request = lax.rem(row, 16)
    for s, out in enumerate(outs):
        first = lax.rem(x + s, NX) * 16
        wanted = jnp.zeros((64, 256), jnp.int32)
        for j in range(16):
            wanted = jnp.where(request == j, owner[first + j], wanted)
        pick = ((wanted == slot) & same_step).astype(F32).astype(BF16)
        out[...] = dot(pick, high) + dot(pick, low)


def project(owner, w, bufs):
    return pl.pallas_call(
        project_kernel,
        out_shape=(jax.ShapeDtypeStruct((64, HD), F32),) * 4,
        in_specs=[SMEM] + [VMEM] * 9,
        out_specs=(VMEM,) * 4,
        compiler_params=params(),
        cost_estimate=cost(1 << 28, 2 << 20),
        name="project",
    )(owner, w, *bufs)


def find_places(owner, lengths, blocks, meta):
    z, y, c = lax.axis_index("z"), lax.axis_index("y"), lax.axis_index("c")
    line = y * NC + c
    root = jnp.int32(0)
    for r in range(SLOTS):
        slot = owner[r]
        meta[jnp.where(slot & 7 == line, slot >> 3, 15)] = lengths[r]
        root = jnp.where(blocks[r] == 0, r, root)
    meta[8] = root // 8
    meta[9] = lax.rem(root, 8) // 2
    meta[10] = lax.rem(root, 2)
    meta[11] = jnp.where(root == z * 8 + line, 1, 0)


def own_kernel(
    q, xk, xv, owner, lengths, blocks, out, lse, meta, values, staged, lse_v, q_v, xk_v, xv_v, owner_s, lengths_s, blocks_s, sems
):
    copies = [(xk, xk_v), (xv, xv_v)]
    for group in range(4):
        lanes = slice(group * 512, (group + 1) * 512)
        copies.append((q.at[:, lanes], q_v.at[:, lanes]))
    copies += [(owner, owner_s), (lengths, lengths_s), (blocks, blocks_s)]
    copies = [pltpu.make_async_copy(src, dst, sems.at[i]) for i, (src, dst) in enumerate(copies)]
    for copy in copies:
        copy.start()
    causal = iota((128, 128), 0) >= iota((128, 128), 1)
    results = []
    for copy in copies[6:]:
        copy.wait()
    find_places(owner_s, lengths_s, blocks_s, meta)
    copies[0].wait()
    copies[1].wait()
    for k in range(2):
        values[k, :, 0:HD] = xv_v[:, k * HD : (k + 1) * HD]
        values[k, :, HD:] = jnp.ones((ROWS, HD), BF16)
    for group in range(4):
        units = [(group * 4 + h, half) for h in range(4) for half in range(2)]
        tiles, tops = [], []
        copies[2 + group].wait()
        for h, half in units:
            near = (half + 1) * 128
            keys = xk_v[0:near, (h // 8) * HD : (h // 8 + 1) * HD]
            own = dot(q_v[near - 128 : near, h * HD : (h + 1) * HD], keys, NT)
            diagonal = jnp.where(causal, own[:, near - 128 :], LOW)
            tiles.append([own[:, :HD], diagonal] if half else [diagonal])
        for parts in tiles:
            tops.append(
                jnp.max(functools.reduce(jnp.maximum, parts), axis=1, keepdims=True) * SCALE2
            )
        for (h, half), parts, top in zip(units, tiles, tops):
            near = (half + 1) * 128
            weights = [jnp.exp2(t * SCALE2 - top).astype(BF16) for t in parts]
            weights = jnp.concatenate(weights, axis=1) if half else weights[0]
            summed = dot(weights, values[h // 8, 0:near, :])
            rows, lanes = slice(near - 128, near), slice(h * HD, (h + 1) * HD)
            staged[rows, lanes] = summed[:, :HD] / summed[:, HD:]
            lse_v[rows, lanes] = top + jnp.log2(summed[:, HD:])
        lanes = slice(group * 512, (group + 1) * 512)
        for i, (src, dst) in enumerate(((staged, out), (lse_v, lse))):
            sem = sems.at[9 + group * 2 + i]
            results.append(pltpu.make_async_copy(src.at[:, lanes], dst.at[:, lanes], sem))
            results[-1].start()
    for copy in results:
        copy.wait()


def context_own(*args):
    args = [pltpu.with_memory_space_constraint(a, pltpu.HBM) for a in args]
    return pl.pallas_call(
        own_kernel,
        out_shape=(
            pltpu.HBM((ROWS, 2048), F32),
            pltpu.HBM((ROWS, 2048), F32),
            jax.ShapeDtypeStruct((16,), jnp.int32),
        ),
        in_specs=[pl.BlockSpec(memory_space=pltpu.HBM)] * 6,
        out_specs=(pl.BlockSpec(memory_space=pltpu.HBM),) * 2 + (SMEM,),
        scratch_shapes=[
            pltpu.VMEM((2, ROWS, 2 * HD), BF16),
            pltpu.VMEM((ROWS, 2048), F32),
            pltpu.VMEM((ROWS, 2048), F32),
            pltpu.VMEM((ROWS, 2048), BF16),
            pltpu.VMEM((ROWS, 256), BF16),
            pltpu.VMEM((ROWS, 256), BF16),
            pltpu.SMEM((SLOTS,), jnp.int32),
            pltpu.SMEM((SLOTS,), jnp.int32),
            pltpu.SMEM((SLOTS,), jnp.int32),
            pltpu.SemaphoreType.DMA((17,)),
        ],
        compiler_params=params(),
        cost_estimate=cost(1 << 30, 6 << 20, 1 << 20),
        name="context_own",
    )(*args)


def far_kernel(meta, q, own, lse, *refs):
    bufs, (out, keys, values, staged, sems) = refs[:8], refs[8:]
    hide = jnp.where(meta[11] == 1, -LOW, 0.0).astype(F32)
    for k in range(2):
        values[k, :, HD:] = jnp.ones((ROWS, HD), BF16)
        for j, buf in enumerate(bufs):
            for half in range(2):
                at, tile = j * 32 + half * 16, k * 2 + half
                keys[k, at : at + 16, :] = buf[tile, 64:80, :]
                values[k, at : at + 16, 0:HD] = buf[4 + tile, 64:80, :]
    copies = []
    for group in range(4):
        k = group // 2
        heads = [slice(h * HD, (h + 1) * HD) for h in range(group * 4, group * 4 + 4)]
        scores = dot(jnp.concatenate([q[:, lanes] for lanes in heads], axis=0), keys[k], NT)
        tiles = [scores[i * ROWS : (i + 1) * ROWS] for i in range(4)]
        tops = [
            jnp.max(jnp.maximum(t[:, :HD], t[:, HD:]), axis=1, keepdims=True) * SCALE2 - hide
            for t in tiles
        ]
        nears = [lse[:, lanes] for lanes in heads]
        tops = [jnp.maximum(top, near) for top, near in zip(tops, nears)]
        weights = []
        for t, top in zip(tiles, tops):
            top = top + hide
            halves = [jnp.exp2(half * SCALE2 - top).astype(BF16) for half in (t[:, :HD], t[:, HD:])]
            weights.append(jnp.concatenate(halves, axis=1))
        summed = dot(jnp.concatenate(weights, axis=0), values[k])
        for i, (top, near, lanes) in enumerate(zip(tops, nears, heads)):
            part = summed[i * ROWS : (i + 1) * ROWS]
            factor = jnp.exp2(near - top)
            joint = part[:, :HD] + factor * own[:, lanes]
            staged[:, lanes] = (joint / (part[:, HD:] + factor)).astype(BF16)
        lanes = slice(group * 512, (group + 1) * 512)
        copies.append(pltpu.make_async_copy(staged.at[:, lanes], out.at[:, lanes], sems.at[group]))
        copies[-1].start()
    for copy in copies:
        copy.wait()


def context_far(meta, q, own, lse, bufs):
    return pl.pallas_call(
        far_kernel,
        out_shape=jax.ShapeDtypeStruct((ROWS, 2048), BF16),
        in_specs=[SMEM] + [VMEM] * 11,
        out_specs=pl.BlockSpec(memory_space=pl.ANY),
        scratch_shapes=[
            pltpu.VMEM((2, ROWS, HD), BF16),
            pltpu.VMEM((2, ROWS, 2 * HD), BF16),
            pltpu.VMEM((ROWS, 2048), BF16),
            pltpu.SemaphoreType.DMA((4,)),
        ],
        compiler_params=params(),
        cost_estimate=cost(1 << 30, 6 << 20, 1 << 20),
        name="context_far",
    )(meta, q, own, lse, *bufs)


def shifted(value, axis, size, shift):
    return lax.ppermute(value, axis, [(i, (i + shift) % size) for i in range(size)])


def on_device(
    ctx_queries,
    ctx_keys,
    ctx_values,
    block_map,
    cache_keys,
    cache_values,
    dec_queries,
    new_keys,
    new_values,
    cache_lengths,
    owner,
    out_weight,
):
    packed, *payloads = prep(
        dec_queries.reshape(STEPS, -1),
        new_keys.reshape(STEPS, -1),
        new_values.reshape(STEPS, -1),
        cache_keys,
        cache_values,
        ctx_keys,
        ctx_values,
    )
    shards = [shifted(payloads[s], "y", NY, s) for s in range(1, NY)]
    gathered = lax.all_to_all(packed, "z", 0, 0, tiled=True)
    own, lse, meta = context_own(ctx_queries, ctx_keys, ctx_values, owner, cache_lengths, block_map)
    q, ro, rm, rl = line_part(gathered)
    q, ro, rm, rl, own, lse, meta, *shards = lax.optimization_barrier(
        (q, ro, rm, rl, own, lse, meta, *shards)
    )
    shards = [payloads[0]] + shards
    state = first_part(meta, q, shards)
    shards = shards + [shifted(b, "c", NC, 1) for b in shards]
    parts = lax.all_to_all(second_part(meta, q, state, shards), "z", 0, 0, tiled=True)
    merged = lax.all_to_all(merge(meta, parts, ro, rm, rl), "z", 0, 0, tiled=True)
    lines = [merged] + [shifted(merged, "y", NY, s) for s in range(1, NY)]
    everything = lines + [shifted(b, "c", NC, 1) for b in lines]
    ctx_out = context_far(meta, ctx_queries, own, lse, everything)
    mine, *others = project(owner, out_weight, everything)
    total = mine
    for s, part in enumerate(others):
        total = total + shifted(part, "x", NX, s + 1)
    dec_out = total.astype(BF16).reshape(STEPS, 16, HD)
    return (ctx_out, dec_out)


def solution(mesh):
    grid = Mesh(mesh.devices.reshape(NZ, NY, NC, NX), ("z", "y", "c", "x"))
    ctx = ("z", "y", "c")
    in_specs = (
        P(ctx, "x"),
        P(ctx, "x"),
        P(ctx, "x"),
        P(),
        P(ctx, "x"),
        P(ctx, "x"),
        P(None, ctx, "x"),
        P(None, ctx, "x"),
        P(None, ctx, "x"),
        P(),
        P(),
        P("x", ctx),
    )
    out_specs = (P(ctx, "x"), P(None, "x", ctx))
    return jax.shard_map(on_device, mesh=grid, in_specs=in_specs, out_specs=out_specs, check_vma=False)
```

```python
import functools
import math

import jax
import jax.numpy as jnp
from jax import lax
from jax.experimental import pallas as pl
from jax.experimental.pallas import tpu as pltpu
from jax.sharding import Mesh, PartitionSpec as P

HD = 128
STEPS = 4
NZ, NY, NC, NX = 8, 4, 2, 4
ROWS = 256
SLOTS = 64
SCALE2 = math.log2(math.e) / math.sqrt(HD)
LOW = -1e29
FLOOR = -(2.0**80)
F32 = jnp.float32
BF16 = jnp.bfloat16
VMEM = pl.BlockSpec(memory_space=pltpu.VMEM)
SMEM = pl.BlockSpec(memory_space=pltpu.SMEM)
NT = (((1,), (1,)), ((), ()))
NN = (((1,), (0,)), ((), ()))


def iota(shape, dim):
    return lax.broadcasted_iota(jnp.int32, shape, dim)


def dot(a, b, dims=NN):
    return lax.dot_general(a, b, dims, preferred_element_type=F32)


def params(mib=16):
    return pltpu.CompilerParams(vmem_limit_bytes=mib * 2**20)


def cost(flops, moved, trans=0):
    return pl.CostEstimate(flops=flops, bytes_accessed=moved, transcendentals=trans)


def prep_kernel(dq, nk, nv, ck, cv, xk, xv, q_out, p0, p1, p2, p3, scratch, dq_v, nk_v, nv_v, xk_v, xv_v, sems):
    y = lax.axis_index("y")
    copies = [
        (dq, dq_v),
        (nk, nk_v),
        (nv, nv_v),
        (ck, p0.at[0:ROWS, :]),
        (cv, p0.at[ROWS : 2 * ROWS, :]),
        (xk, xk_v),
        (xv, xv_v),
    ]
    copies = [pltpu.make_async_copy(src, dst, sems.at[i]) for i, (src, dst) in enumerate(copies)]
    for copy in copies:
        copy.start()
    scratch[...] = jnp.zeros_like(scratch)
    row, col = iota((80, 160), 0), iota((80, 160), 1)
    pick = (col == (row // 4) * 8 + row % 4).astype(F32).astype(BF16)
    for copy in copies[:3]:
        copy.wait()
    for h in range(16):
        scratch[h * 8 : h * 8 + 4, :] = dq_v[:, h * HD : (h + 1) * HD].astype(F32)
    for i, ref in enumerate((nk_v, nv_v)):
        for k in range(2):
            at = 128 + (i * 2 + k) * 8
            scratch[at : at + 4, :] = ref[:, k * HD : (k + 1) * HD].astype(F32)
    packed = dot(pick, scratch[...].astype(BF16)).astype(BF16)
    for s in range(NZ):
        q_out[s] = packed
    for copy in copies[3:]:
        copy.wait()
    shard = p0[0 : 2 * ROWS, :]
    for out in (p1, p2, p3):
        out[0 : 2 * ROWS, :] = shard
    for s, out in enumerate((p0, p1, p2, p3)):
        for i in range(8):
            source, k = (xk_v, xv_v)[i // 4], (i % 4) // 2
            for core in range(2):
                at = lax.rem(y + s, NY) * 64 + core * 32 + (i % 2) * 16
                tile = source[pl.ds(pl.multiple_of(at, 16), 16), k * HD : (k + 1) * HD]
                out[512 + i * 16 : 528 + i * 16, core * HD : (core + 1) * HD] = tile


def prep(*args):
    args = [pltpu.with_memory_space_constraint(a, pltpu.HBM) for a in args]
    payload = jax.ShapeDtypeStruct((640, 256), BF16)
    return pl.pallas_call(
        prep_kernel,
        out_shape=(jax.ShapeDtypeStruct((NZ, 80, HD), BF16),) + (payload,) * 4,
        in_specs=[pl.BlockSpec(memory_space=pltpu.HBM)] * 7,
        out_specs=(VMEM,) * 5,
        scratch_shapes=[
            pltpu.VMEM((160, HD), F32),
            pltpu.VMEM((STEPS, 2048), BF16),
            pltpu.VMEM((STEPS, 256), BF16),
            pltpu.VMEM((STEPS, 256), BF16),
            pltpu.VMEM((ROWS, 256), BF16),
            pltpu.VMEM((ROWS, 256), BF16),
            pltpu.SemaphoreType.DMA((7,)),
        ],
        compiler_params=params(),
        cost_estimate=cost(1 << 20, 1 << 20),
        name="prep",
    )(*args)


def line_kernel(g, q_out, ro_out, rm_out, rl_out):
    z = lax.axis_index("z")
    row, col = iota((256, 256), 0), iota((256, 256), 1)
    source = lax.rem(row // 4, 8) * 32 + (row // 32) * 4 + lax.rem(row, 4)
    pick = (col == source).astype(F32).astype(BF16)
    for k in range(2):
        natural = jnp.concatenate([g[s, k * 32 : (k + 1) * 32, :] for s in range(NZ)], axis=0)
        q_out[k * 256 : (k + 1) * 256, :] = dot(pick, natural).astype(BF16)
    mine = q_out[pl.ds(pl.multiple_of(z * 64, 64), 64), :]
    tokens = jnp.concatenate([g[s, 64:80, :] for s in range(NZ)], axis=0)
    wide = tokens.astype(F32)
    values = jnp.concatenate([wide[8:], wide[:8]], axis=0).astype(BF16)
    scores = dot(mine, tokens, NT) * SCALE2
    row, col = iota((64, 128), 0), iota((64, 128), 1)
    seen = (
        (lax.rem(row // 4, 8) == col // 16)
        & (lax.rem(col, 16) // 4 == z // 4)
        & (lax.rem(col, 4) <= lax.rem(row, 4))
    )
    scores = jnp.where(seen, scores, LOW)
    top = jnp.max(scores, axis=1, keepdims=True)
    weights = jnp.exp2(scores - top)
    rm_out[...] = jnp.broadcast_to(top, (64, HD))
    rl_out[...] = jnp.broadcast_to(jnp.sum(weights, axis=1, keepdims=True), (64, HD))
    ro_out[...] = dot(weights.astype(BF16), values)


def line_part(gathered):
    part = jax.ShapeDtypeStruct((64, HD), F32)
    return pl.pallas_call(
        line_kernel,
        out_shape=(jax.ShapeDtypeStruct((512, HD), BF16), part, part, part),
        in_specs=[VMEM],
        out_specs=(VMEM,) * 4,
        compiler_params=params(),
        cost_estimate=cost(1 << 24, 1 << 20),
        name="line_part",
    )(gathered)


def shard_scores(meta, q, bufs, k, core, scores):
    z, y = lax.axis_index("z"), lax.axis_index("y")
    rowslot = iota((32, HD), 0) // 4
    length = jnp.zeros((32, HD), jnp.int32)
    for s in range(8):
        length = jnp.where(rowslot == s, meta[s], length)
    lane = iota((32, HD), 1)
    tops = []
    for b in range(4):
        room = length - (z * 8 + lax.rem(y - b + NY, NY) * NC + core) * ROWS
        keep = jnp.concatenate([lane < room, lane + HD < room], axis=1)
        raw = dot(q[k * 256 : (k + 1) * 256, :], bufs[b][0:ROWS, k * HD : (k + 1) * HD], NT)
        raw = jnp.where(keep[None], raw.reshape(8, 32, 256), LOW).reshape(256, 256)
        scores[k, b] = raw
        tops.append(jnp.max(jnp.maximum(raw[:, :HD], raw[:, HD:]), axis=1, keepdims=True))
    return tops


def shard_sums(bufs, k, tops, top, scores, total, weighted):
    for b in range(4):
        weights = jnp.exp2((scores[k, b] - tops[b]) * SCALE2)
        factor = jnp.exp2(tops[b] * SCALE2 - top)
        total = total + (weights[:, :HD] + weights[:, HD:]) * factor
        weighted = weighted + factor * dot(
            weights.astype(BF16), bufs[b][ROWS : 2 * ROWS, k * HD : (k + 1) * HD]
        )
    return total, weighted


def first_kernel(meta, q, *refs):
    bufs, (o_out, m_out, l_out, scores) = refs[:4], refs[4:]
    core = lax.axis_index("c")
    tops = [shard_scores(meta, q, bufs, k, core, scores) for k in range(2)]
    zeros = jnp.zeros((256, HD), F32)
    for k in range(2):
        rows = slice(k * 256, (k + 1) * 256)
        top = jnp.maximum(functools.reduce(jnp.maximum, tops[k]) * SCALE2, FLOOR)
        l_out[rows, :], o_out[rows, :] = shard_sums(bufs, k, tops[k], top, scores, zeros, zeros)
        m_out[rows, :] = jnp.broadcast_to(top, (256, HD))


def first_part(meta, q, bufs):
    part = jax.ShapeDtypeStruct((512, HD), F32)
    return pl.pallas_call(
        first_kernel,
        out_shape=(part,) * 3,
        in_specs=[SMEM] + [VMEM] * 5,
        out_specs=(VMEM,) * 3,
        scratch_shapes=[pltpu.VMEM((2, 4, 256, 256), F32)],
        compiler_params=params(),
        cost_estimate=cost(1 << 29, 2 << 20, 1 << 19),
        name="first_part",
    )(meta, q, *bufs)


def second_kernel(meta, q, o, m, l, *refs):
    all_bufs, bufs, (out, scores) = refs[:8], refs[4:8], refs[8:]
    core = 1 - lax.axis_index("c")
    tops = [shard_scores(meta, q, bufs, k, core, scores) for k in range(2)]
    column = iota((256, HD), 1)
    for k in range(2):
        rows = slice(k * 256, (k + 1) * 256)
        top = jnp.maximum(functools.reduce(jnp.maximum, tops[k]) * SCALE2, m[rows, :])
        top = top.astype(BF16).astype(F32)
        factor = jnp.exp2(m[rows, :] - top)
        total, weighted = shard_sums(
            bufs, k, tops[k], top, scores, l[rows, :] * factor, o[rows, :] * factor
        )
        total = jnp.sum(total, axis=1, keepdims=True)
        total_high = total.astype(BF16).astype(F32)
        total_low = total - total_high
        stats = jnp.where(
            column == 0, top, jnp.where(column == 1, total_high, jnp.where(column == 2, total_low, 0.0))
        )
        weighted = weighted.astype(BF16)
        for pair in range(2):
            flipped = jnp.transpose(stats[pair * 128 : (pair + 1) * 128])[:16].astype(BF16)
            out[k * 4 + pair * 2, 64:80, :] = flipped
            out[k * 4 + pair * 2 + 1, 64:80, :] = flipped
        for part in range(4):
            out[k * 4 + part, 0:64, :] = weighted[part * 64 : (part + 1) * 64]
    y, c = lax.axis_index("y"), lax.axis_index("c")
    root_shift = lax.rem(y - meta[9] + NY, NY)
    for b in range(8):
        for lane_half in range(2):
            swapped = b // 4
            from_core = jnp.where(meta[10] == c, 0, 1)

            @pl.when((root_shift == b % 4) & (from_core == swapped) & (c == lane_half))
            def _(b=b, lane_half=lane_half):
                lanes = slice(lane_half * HD, (lane_half + 1) * HD)
                for piece in range(NZ):
                    out[piece, 80:96, :] = all_bufs[b][512 + piece * 16 : 528 + piece * 16, lanes]


def second_part(meta, q, state, bufs):
    return pl.pallas_call(
        second_kernel,
        out_shape=jax.ShapeDtypeStruct((NZ, 96, HD), BF16),
        in_specs=[SMEM] + [VMEM] * 12,
        out_specs=VMEM,
        scratch_shapes=[pltpu.VMEM((2, 4, 256, 256), F32)],
        compiler_params=params(),
        cost_estimate=cost(1 << 29, 2 << 20, 1 << 19),
        name="second_part",
    )(meta, q, *state, *bufs)


def merge_kernel(meta, parts, ro, rm, rl, out, scratch):
    z = lax.axis_index("z")
    stats = jnp.concatenate([parts[j, 64:80, :] for j in range(NZ)], axis=0).astype(F32)
    scratch[...] = jnp.transpose(stats)
    mine = scratch[pl.ds(pl.multiple_of(lax.rem(z, 2) * 64, 64), 64), :]
    tops = [mine[:, j * 16 : j * 16 + 1] for j in range(NZ)]
    totals = [mine[:, j * 16 + 1 : j * 16 + 2] + mine[:, j * 16 + 2 : j * 16 + 3] for j in range(NZ)]
    top = rm[...]
    for t in tops:
        top = jnp.maximum(top, t)
    factor = jnp.exp2(rm[...] - top)
    total = rl[...] * factor
    weighted = ro[...] * factor
    for j in range(NZ):
        factor = jnp.exp2(tops[j] - top)
        total = total + totals[j] * factor
        weighted = weighted + parts[j, 0:64, :].astype(F32) * factor
    attention = (weighted / total).astype(BF16)
    anchor = parts[meta[8], 80:96, :]
    for s in range(NZ):
        out[s, 0:64, :] = attention
        out[s, 64:80, :] = anchor


def merge(meta, parts, ro, rm, rl):
    return pl.pallas_call(
        merge_kernel,
        out_shape=jax.ShapeDtypeStruct((NZ, 80, HD), BF16),
        in_specs=[SMEM] + [VMEM] * 4,
        out_specs=VMEM,
        scratch_shapes=[pltpu.VMEM((HD, HD), F32)],
        compiler_params=params(),
        cost_estimate=cost(1 << 20, 1 << 19),
        name="merge",
    )(meta, parts, ro, rm, rl)


def picks_kernel(owner, out):
    y, c, x = lax.axis_index("y"), lax.axis_index("c"), lax.axis_index("x")
    col = iota((64, 256), 1)
    buf = col // 32
    slot = (
        lax.rem(col // 4, 8) * 8
        + lax.rem(y - lax.rem(buf, 4) + NY, NY) * NC
        + jnp.where(buf >= 4, 1 - c, c)
    )
    row = iota((64, 256), 0)
    same_step = lax.rem(col, 4) == row // 16
    request = lax.rem(row, 16)
    for s in range(NX):
        first = lax.rem(x + s, NX) * 16
        wanted = jnp.zeros((64, 256), jnp.int32)
        for j in range(16):
            wanted = jnp.where(request == j, owner[first + j], wanted)
        out[s] = ((wanted == slot) & same_step).astype(F32).astype(BF16)


def make_picks(owner):
    return pl.pallas_call(
        picks_kernel,
        out_shape=jax.ShapeDtypeStruct((NX, 64, 256), BF16),
        in_specs=[SMEM],
        out_specs=VMEM,
        compiler_params=params(),
        cost_estimate=cost(1 << 22, 1 << 18),
        name="picks",
    )(owner)


def line_product(w, bufs):
    total = jnp.zeros((128, HD), F32)
    for zz in range(NZ):
        left = jnp.concatenate([b[zz, 0:32, :] for b in bufs], axis=0)
        right = jnp.concatenate([b[zz, 32:64, :] for b in bufs], axis=0)
        total = total + dot(
            jnp.concatenate([left, right], axis=1), w[zz * 256 : (zz + 1) * 256, :]
        )
    high = total.astype(BF16)
    return high, (total - high.astype(F32)).astype(BF16)


def near_kernel(w, *refs):
    refs[4][0], refs[4][1] = line_product(w, refs[:4])


def project_near(w, bufs):
    return pl.pallas_call(
        near_kernel,
        out_shape=jax.ShapeDtypeStruct((2, 128, HD), BF16),
        in_specs=[VMEM] * 5,
        out_specs=VMEM,
        compiler_params=params(),
        cost_estimate=cost(1 << 26, 1 << 20),
        name="project_near",
    )(w, *bufs)


def project_kernel(picks, near, w, *refs):
    bufs, outs = refs[:4], refs[4:8]
    high, low = line_product(w, bufs)
    high = jnp.concatenate([near[0], high], axis=0)
    low = jnp.concatenate([near[1], low], axis=0)
    for s, out in enumerate(outs):
        out[...] = dot(picks[s], high) + dot(picks[s], low)


def project(picks, near, w, bufs):
    return pl.pallas_call(
        project_kernel,
        out_shape=(jax.ShapeDtypeStruct((64, HD), F32),) * 4,
        in_specs=[VMEM] * 7,
        out_specs=(VMEM,) * 4,
        compiler_params=params(),
        cost_estimate=cost(1 << 27, 2 << 20),
        name="project",
    )(picks, near, w, *bufs)


def find_places(owner, lengths, blocks, meta):
    z, y, c = lax.axis_index("z"), lax.axis_index("y"), lax.axis_index("c")
    line = y * NC + c
    root = jnp.int32(0)
    for r in range(SLOTS):
        slot = owner[r]
        meta[jnp.where(slot & 7 == line, slot >> 3, 15)] = lengths[r]
        root = jnp.where(blocks[r] == 0, r, root)
    meta[8] = root // 8
    meta[9] = lax.rem(root, 8) // 2
    meta[10] = lax.rem(root, 2)
    meta[11] = jnp.where(root == z * 8 + line, 1, 0)


def own_kernel(
    q, xk, xv, owner, lengths, blocks, out, lse, meta, values, staged, lse_v, q_v, xk_v, xv_v, owner_s, lengths_s, blocks_s, sems
):
    copies = [(xk, xk_v), (xv, xv_v)]
    for group in range(4):
        lanes = slice(group * 512, (group + 1) * 512)
        copies.append((q.at[:, lanes], q_v.at[:, lanes]))
    copies += [(owner, owner_s), (lengths, lengths_s), (blocks, blocks_s)]
    copies = [pltpu.make_async_copy(src, dst, sems.at[i]) for i, (src, dst) in enumerate(copies)]
    for copy in copies:
        copy.start()
    causal = iota((128, 128), 0) >= iota((128, 128), 1)
    results = []
    for copy in copies[6:]:
        copy.wait()
    find_places(owner_s, lengths_s, blocks_s, meta)
    copies[0].wait()
    copies[1].wait()
    for k in range(2):
        values[k, :, 0:HD] = xv_v[:, k * HD : (k + 1) * HD]
        values[k, :, HD:] = jnp.ones((ROWS, HD), BF16)
    for group in range(4):
        units = [(group * 4 + h, half) for h in range(4) for half in range(2)]
        tiles, tops = [], []
        copies[2 + group].wait()
        for h, half in units:
            near = (half + 1) * 128
            keys = xk_v[0:near, (h // 8) * HD : (h // 8 + 1) * HD]
            own = dot(q_v[near - 128 : near, h * HD : (h + 1) * HD], keys, NT)
            diagonal = jnp.where(causal, own[:, near - 128 :], LOW)
            tiles.append([own[:, :HD], diagonal] if half else [diagonal])
        for parts in tiles:
            tops.append(
                jnp.max(functools.reduce(jnp.maximum, parts), axis=1, keepdims=True) * SCALE2
            )
        for (h, half), parts, top in zip(units, tiles, tops):
            near = (half + 1) * 128
            weights = [jnp.exp2(t * SCALE2 - top).astype(BF16) for t in parts]
            weights = jnp.concatenate(weights, axis=1) if half else weights[0]
            summed = dot(weights, values[h // 8, 0:near, :])
            rows, lanes = slice(near - 128, near), slice(h * HD, (h + 1) * HD)
            staged[rows, lanes] = summed[:, :HD] / summed[:, HD:]
            lse_v[rows, lanes] = top + jnp.log2(summed[:, HD:])
        lanes = slice(group * 512, (group + 1) * 512)
        for i, (src, dst) in enumerate(((staged, out), (lse_v, lse))):
            sem = sems.at[9 + group * 2 + i]
            results.append(pltpu.make_async_copy(src.at[:, lanes], dst.at[:, lanes], sem))
            results[-1].start()
    for copy in results:
        copy.wait()


def context_own(*args):
    args = [pltpu.with_memory_space_constraint(a, pltpu.HBM) for a in args]
    return pl.pallas_call(
        own_kernel,
        out_shape=(
            pltpu.HBM((ROWS, 2048), F32),
            pltpu.HBM((ROWS, 2048), F32),
            jax.ShapeDtypeStruct((16,), jnp.int32),
        ),
        in_specs=[pl.BlockSpec(memory_space=pltpu.HBM)] * 6,
        out_specs=(pl.BlockSpec(memory_space=pltpu.HBM),) * 2 + (SMEM,),
        scratch_shapes=[
            pltpu.VMEM((2, ROWS, 2 * HD), BF16),
            pltpu.VMEM((ROWS, 2048), F32),
            pltpu.VMEM((ROWS, 2048), F32),
            pltpu.VMEM((ROWS, 2048), BF16),
            pltpu.VMEM((ROWS, 256), BF16),
            pltpu.VMEM((ROWS, 256), BF16),
            pltpu.SMEM((SLOTS,), jnp.int32),
            pltpu.SMEM((SLOTS,), jnp.int32),
            pltpu.SMEM((SLOTS,), jnp.int32),
            pltpu.SemaphoreType.DMA((17,)),
        ],
        compiler_params=params(),
        cost_estimate=cost(1 << 30, 6 << 20, 1 << 20),
        name="context_own",
    )(*args)


def far_kernel(meta, q, own, lse, *refs):
    bufs, (out, keys, values, staged, sems) = refs[:8], refs[8:]
    hide = jnp.where(meta[11] == 1, -LOW, 0.0).astype(F32)
    for k in range(2):
        values[k, :, HD:] = jnp.ones((ROWS, HD), BF16)
        for j, buf in enumerate(bufs):
            for half in range(2):
                at, tile = j * 32 + half * 16, k * 2 + half
                keys[k, at : at + 16, :] = buf[tile, 64:80, :]
                values[k, at : at + 16, 0:HD] = buf[4 + tile, 64:80, :]
    copies = []
    for group in range(4):
        k = group // 2
        heads = [slice(h * HD, (h + 1) * HD) for h in range(group * 4, group * 4 + 4)]
        scores = dot(jnp.concatenate([q[:, lanes] for lanes in heads], axis=0), keys[k], NT)
        tiles = [scores[i * ROWS : (i + 1) * ROWS] for i in range(4)]
        tops = [
            jnp.max(jnp.maximum(t[:, :HD], t[:, HD:]), axis=1, keepdims=True) * SCALE2 - hide
            for t in tiles
        ]
        nears = [lse[:, lanes] for lanes in heads]
        tops = [jnp.maximum(top, near) for top, near in zip(tops, nears)]
        weights = []
        for t, top in zip(tiles, tops):
            top = top + hide
            halves = [jnp.exp2(half * SCALE2 - top).astype(BF16) for half in (t[:, :HD], t[:, HD:])]
            weights.append(jnp.concatenate(halves, axis=1))
        summed = dot(jnp.concatenate(weights, axis=0), values[k])
        for i, (top, near, lanes) in enumerate(zip(tops, nears, heads)):
            part = summed[i * ROWS : (i + 1) * ROWS]
            factor = jnp.exp2(near - top)
            joint = part[:, :HD] + factor * own[:, lanes]
            staged[:, lanes] = (joint / (part[:, HD:] + factor)).astype(BF16)
        lanes = slice(group * 512, (group + 1) * 512)
        copies.append(pltpu.make_async_copy(staged.at[:, lanes], out.at[:, lanes], sems.at[group]))
        copies[-1].start()
    for copy in copies:
        copy.wait()


def context_far(meta, q, own, lse, bufs):
    return pl.pallas_call(
        far_kernel,
        out_shape=jax.ShapeDtypeStruct((ROWS, 2048), BF16),
        in_specs=[SMEM] + [VMEM] * 11,
        out_specs=pl.BlockSpec(memory_space=pl.ANY),
        scratch_shapes=[
            pltpu.VMEM((2, ROWS, HD), BF16),
            pltpu.VMEM((2, ROWS, 2 * HD), BF16),
            pltpu.VMEM((ROWS, 2048), BF16),
            pltpu.SemaphoreType.DMA((4,)),
        ],
        compiler_params=params(),
        cost_estimate=cost(1 << 30, 6 << 20, 1 << 20),
        name="context_far",
    )(meta, q, own, lse, *bufs)


def shifted(value, axis, size, shift):
    return lax.ppermute(value, axis, [(i, (i + shift) % size) for i in range(size)])


def on_device(
    ctx_queries,
    ctx_keys,
    ctx_values,
    block_map,
    cache_keys,
    cache_values,
    dec_queries,
    new_keys,
    new_values,
    cache_lengths,
    owner,
    out_weight,
):
    packed, *payloads = prep(
        dec_queries.reshape(STEPS, -1),
        new_keys.reshape(STEPS, -1),
        new_values.reshape(STEPS, -1),
        cache_keys,
        cache_values,
        ctx_keys,
        ctx_values,
    )
    shards = [shifted(payloads[s], "y", NY, s) for s in range(1, NY)]
    gathered = lax.all_to_all(packed, "z", 0, 0, tiled=True)
    own, lse, meta = context_own(ctx_queries, ctx_keys, ctx_values, owner, cache_lengths, block_map)
    q, ro, rm, rl = line_part(gathered)
    q, ro, rm, rl, own, lse, meta, *shards = lax.optimization_barrier(
        (q, ro, rm, rl, own, lse, meta, *shards)
    )
    shards = [payloads[0]] + shards
    state = first_part(meta, q, shards)
    shards = shards + [shifted(b, "c", NC, 1) for b in shards]
    parts = lax.all_to_all(second_part(meta, q, state, shards), "z", 0, 0, tiled=True)
    merged = lax.all_to_all(merge(meta, parts, ro, rm, rl), "z", 0, 0, tiled=True)
    merged, owner = lax.optimization_barrier((merged, owner))
    picks = make_picks(owner)
    lines = [merged] + [shifted(merged, "y", NY, s) for s in range(1, NY)]
    swapped = [shifted(b, "c", NC, 1) for b in lines]
    near = project_near(out_weight, lines)
    mine, *others = project(picks, near, out_weight, swapped)
    ctx_out = context_far(meta, ctx_queries, own, lse, lines + swapped)
    total = mine
    for s, part in enumerate(others):
        total = total + shifted(part, "x", NX, s + 1)
    dec_out = total.astype(BF16).reshape(STEPS, 16, HD)
    return (ctx_out, dec_out)


def solution(mesh):
    grid = Mesh(mesh.devices.reshape(NZ, NY, NC, NX), ("z", "y", "c", "x"))
    ctx = ("z", "y", "c")
    in_specs = (
        P(ctx, "x"),
        P(ctx, "x"),
        P(ctx, "x"),
        P(),
        P(ctx, "x"),
        P(ctx, "x"),
        P(None, ctx, "x"),
        P(None, ctx, "x"),
        P(None, ctx, "x"),
        P(),
        P(),
        P("x", ctx),
    )
    out_specs = (P(ctx, "x"), P(None, "x", ctx))
    return jax.shard_map(on_device, mesh=grid, in_specs=in_specs, out_specs=out_specs, check_vma=False)
```

```python
import functools
import math

import jax
import jax.numpy as jnp
from jax import lax
from jax.experimental import pallas as pl
from jax.experimental.pallas import tpu as pltpu
from jax.sharding import Mesh, PartitionSpec as P

HD = 128
STEPS = 4
NZ, NY, NC, NX = 8, 4, 2, 4
ROWS = 256
SLOTS = 64
SCALE2 = math.log2(math.e) / math.sqrt(HD)
LOW = -1e29
FLOOR = -(2.0**80)
F32 = jnp.float32
BF16 = jnp.bfloat16
VMEM = pl.BlockSpec(memory_space=pltpu.VMEM)
SMEM = pl.BlockSpec(memory_space=pltpu.SMEM)
NT = (((1,), (1,)), ((), ()))
NN = (((1,), (0,)), ((), ()))


def iota(shape, dim):
    return lax.broadcasted_iota(jnp.int32, shape, dim)


def dot(a, b, dims=NN):
    return lax.dot_general(a, b, dims, preferred_element_type=F32)


def params(mib=16):
    return pltpu.CompilerParams(vmem_limit_bytes=mib * 2**20)


def cost(flops, moved, trans=0):
    return pl.CostEstimate(flops=flops, bytes_accessed=moved, transcendentals=trans)


def prep_kernel(dq, nk, nv, ck, cv, xk, xv, q_out, p0, p1, p2, p3, scratch, dq_v, nk_v, nv_v, xk_v, xv_v, sems):
    y = lax.axis_index("y")
    copies = [
        (dq, dq_v),
        (nk, nk_v),
        (nv, nv_v),
        (ck, p0.at[0:ROWS, :]),
        (cv, p0.at[ROWS : 2 * ROWS, :]),
        (xk, xk_v),
        (xv, xv_v),
    ]
    copies = [pltpu.make_async_copy(src, dst, sems.at[i]) for i, (src, dst) in enumerate(copies)]
    for copy in copies:
        copy.start()
    scratch[...] = jnp.zeros_like(scratch)
    row, col = iota((80, 160), 0), iota((80, 160), 1)
    pick = (col == (row // 4) * 8 + row % 4).astype(F32).astype(BF16)
    for copy in copies[:3]:
        copy.wait()
    for h in range(16):
        scratch[h * 8 : h * 8 + 4, :] = dq_v[:, h * HD : (h + 1) * HD].astype(F32)
    for i, ref in enumerate((nk_v, nv_v)):
        for k in range(2):
            at = 128 + (i * 2 + k) * 8
            scratch[at : at + 4, :] = ref[:, k * HD : (k + 1) * HD].astype(F32)
    packed = dot(pick, scratch[...].astype(BF16)).astype(BF16)
    for s in range(NZ):
        q_out[s] = packed
    for copy in copies[3:]:
        copy.wait()
    shard = p0[0 : 2 * ROWS, :]
    for out in (p1, p2, p3):
        out[0 : 2 * ROWS, :] = shard
    for s, out in enumerate((p0, p1, p2, p3)):
        for i in range(8):
            source, k = (xk_v, xv_v)[i // 4], (i % 4) // 2
            for core in range(2):
                at = lax.rem(y + s, NY) * 64 + core * 32 + (i % 2) * 16
                tile = source[pl.ds(pl.multiple_of(at, 16), 16), k * HD : (k + 1) * HD]
                out[512 + i * 16 : 528 + i * 16, core * HD : (core + 1) * HD] = tile


def prep(*args):
    args = [pltpu.with_memory_space_constraint(a, pltpu.HBM) for a in args]
    payload = jax.ShapeDtypeStruct((640, 256), BF16)
    return pl.pallas_call(
        prep_kernel,
        out_shape=(jax.ShapeDtypeStruct((NZ, 80, HD), BF16),) + (payload,) * 4,
        in_specs=[pl.BlockSpec(memory_space=pltpu.HBM)] * 7,
        out_specs=(VMEM,) * 5,
        scratch_shapes=[
            pltpu.VMEM((160, HD), F32),
            pltpu.VMEM((STEPS, 2048), BF16),
            pltpu.VMEM((STEPS, 256), BF16),
            pltpu.VMEM((STEPS, 256), BF16),
            pltpu.VMEM((ROWS, 256), BF16),
            pltpu.VMEM((ROWS, 256), BF16),
            pltpu.SemaphoreType.DMA((7,)),
        ],
        compiler_params=params(),
        cost_estimate=cost(1 << 20, 1 << 20),
        name="prep",
    )(*args)


def line_kernel(g, q_out, ro_out, rm_out, rl_out):
    z = lax.axis_index("z")
    row, col = iota((256, 256), 0), iota((256, 256), 1)
    source = lax.rem(row // 4, 8) * 32 + (row // 32) * 4 + lax.rem(row, 4)
    pick = (col == source).astype(F32).astype(BF16)
    for k in range(2):
        natural = jnp.concatenate([g[s, k * 32 : (k + 1) * 32, :] for s in range(NZ)], axis=0)
        q_out[k * 256 : (k + 1) * 256, :] = dot(pick, natural).astype(BF16)
    mine = q_out[pl.ds(pl.multiple_of(z * 64, 64), 64), :]
    tokens = jnp.concatenate([g[s, 64:80, :] for s in range(NZ)], axis=0)
    wide = tokens.astype(F32)
    values = jnp.concatenate([wide[8:], wide[:8]], axis=0).astype(BF16)
    scores = dot(mine, tokens, NT) * SCALE2
    row, col = iota((64, 128), 0), iota((64, 128), 1)
    seen = (
        (lax.rem(row // 4, 8) == col // 16)
        & (lax.rem(col, 16) // 4 == z // 4)
        & (lax.rem(col, 4) <= lax.rem(row, 4))
    )
    scores = jnp.where(seen, scores, LOW)
    top = jnp.max(scores, axis=1, keepdims=True)
    weights = jnp.exp2(scores - top)
    rm_out[...] = jnp.broadcast_to(top, (64, HD))
    rl_out[...] = jnp.broadcast_to(jnp.sum(weights, axis=1, keepdims=True), (64, HD))
    ro_out[...] = dot(weights.astype(BF16), values)


def line_part(gathered):
    part = jax.ShapeDtypeStruct((64, HD), F32)
    return pl.pallas_call(
        line_kernel,
        out_shape=(jax.ShapeDtypeStruct((512, HD), BF16), part, part, part),
        in_specs=[VMEM],
        out_specs=(VMEM,) * 4,
        compiler_params=params(),
        cost_estimate=cost(1 << 24, 1 << 20),
        name="line_part",
    )(gathered)


def shard_scores(meta, q, bufs, k, core, scores):
    z, y = lax.axis_index("z"), lax.axis_index("y")
    rowslot = iota((32, HD), 0) // 4
    length = jnp.zeros((32, HD), jnp.int32)
    for s in range(8):
        length = jnp.where(rowslot == s, meta[s], length)
    lane = iota((32, HD), 1)
    tops = []
    for b in range(4):
        room = length - (z * 8 + lax.rem(y - b + NY, NY) * NC + core) * ROWS
        keep = jnp.concatenate([lane < room, lane + HD < room], axis=1)
        raw = dot(q[k * 256 : (k + 1) * 256, :], bufs[b][0:ROWS, k * HD : (k + 1) * HD], NT)
        raw = jnp.where(keep[None], raw.reshape(8, 32, 256), LOW).reshape(256, 256)
        scores[k, b] = raw
        tops.append(jnp.max(jnp.maximum(raw[:, :HD], raw[:, HD:]), axis=1, keepdims=True))
    return tops


def shard_sums(bufs, k, tops, top, scores, total, weighted):
    for b in range(4):
        weights = jnp.exp2((scores[k, b] - tops[b]) * SCALE2)
        factor = jnp.exp2(tops[b] * SCALE2 - top)
        total = total + (weights[:, :HD] + weights[:, HD:]) * factor
        weighted = weighted + factor * dot(
            weights.astype(BF16), bufs[b][ROWS : 2 * ROWS, k * HD : (k + 1) * HD]
        )
    return total, weighted


def first_kernel(meta, q, *refs):
    bufs, (o_out, m_out, l_out, scores) = refs[:4], refs[4:]
    core = lax.axis_index("c")
    tops = [shard_scores(meta, q, bufs, k, core, scores) for k in range(2)]
    zeros = jnp.zeros((256, HD), F32)
    for k in range(2):
        rows = slice(k * 256, (k + 1) * 256)
        top = jnp.maximum(functools.reduce(jnp.maximum, tops[k]) * SCALE2, FLOOR)
        l_out[rows, :], o_out[rows, :] = shard_sums(bufs, k, tops[k], top, scores, zeros, zeros)
        m_out[rows, :] = jnp.broadcast_to(top, (256, HD))


def first_part(meta, q, bufs):
    part = jax.ShapeDtypeStruct((512, HD), F32)
    return pl.pallas_call(
        first_kernel,
        out_shape=(part,) * 3,
        in_specs=[SMEM] + [VMEM] * 5,
        out_specs=(VMEM,) * 3,
        scratch_shapes=[pltpu.VMEM((2, 4, 256, 256), F32)],
        compiler_params=params(),
        cost_estimate=cost(1 << 29, 2 << 20, 1 << 19),
        name="first_part",
    )(meta, q, *bufs)


def second_kernel(meta, q, o, m, l, *refs):
    all_bufs, bufs, (out, scores) = refs[:8], refs[4:8], refs[8:]
    core = 1 - lax.axis_index("c")
    tops = [shard_scores(meta, q, bufs, k, core, scores) for k in range(2)]
    column = iota((256, HD), 1)
    for k in range(2):
        rows = slice(k * 256, (k + 1) * 256)
        top = jnp.maximum(functools.reduce(jnp.maximum, tops[k]) * SCALE2, m[rows, :])
        top = top.astype(BF16).astype(F32)
        factor = jnp.exp2(m[rows, :] - top)
        total, weighted = shard_sums(
            bufs, k, tops[k], top, scores, l[rows, :] * factor, o[rows, :] * factor
        )
        total = jnp.sum(total, axis=1, keepdims=True)
        total_high = total.astype(BF16).astype(F32)
        total_low = total - total_high
        stats = jnp.where(
            column == 0, top, jnp.where(column == 1, total_high, jnp.where(column == 2, total_low, 0.0))
        )
        weighted = weighted.astype(BF16)
        for pair in range(2):
            flipped = jnp.transpose(stats[pair * 128 : (pair + 1) * 128])[:16].astype(BF16)
            out[k * 4 + pair * 2, 64:80, :] = flipped
            out[k * 4 + pair * 2 + 1, 64:80, :] = flipped
        for part in range(4):
            out[k * 4 + part, 0:64, :] = weighted[part * 64 : (part + 1) * 64]
    y, c = lax.axis_index("y"), lax.axis_index("c")
    root_shift = lax.rem(y - meta[9] + NY, NY)
    for b in range(8):
        for lane_half in range(2):
            swapped = b // 4
            from_core = jnp.where(meta[10] == c, 0, 1)

            @pl.when((root_shift == b % 4) & (from_core == swapped) & (c == lane_half))
            def _(b=b, lane_half=lane_half):
                lanes = slice(lane_half * HD, (lane_half + 1) * HD)
                for piece in range(NZ):
                    out[piece, 80:96, :] = all_bufs[b][512 + piece * 16 : 528 + piece * 16, lanes]


def second_part(meta, q, state, bufs):
    return pl.pallas_call(
        second_kernel,
        out_shape=jax.ShapeDtypeStruct((NZ, 96, HD), BF16),
        in_specs=[SMEM] + [VMEM] * 12,
        out_specs=VMEM,
        scratch_shapes=[pltpu.VMEM((2, 4, 256, 256), F32)],
        compiler_params=params(),
        cost_estimate=cost(1 << 29, 2 << 20, 1 << 19),
        name="second_part",
    )(meta, q, *state, *bufs)


def merge_kernel(meta, parts, ro, rm, rl, out, scratch):
    z = lax.axis_index("z")
    stats = jnp.concatenate([parts[j, 64:80, :] for j in range(NZ)], axis=0).astype(F32)
    scratch[...] = jnp.transpose(stats)
    mine = scratch[pl.ds(pl.multiple_of(lax.rem(z, 2) * 64, 64), 64), :]
    tops = [mine[:, j * 16 : j * 16 + 1] for j in range(NZ)]
    totals = [mine[:, j * 16 + 1 : j * 16 + 2] + mine[:, j * 16 + 2 : j * 16 + 3] for j in range(NZ)]
    top = rm[...]
    for t in tops:
        top = jnp.maximum(top, t)
    factor = jnp.exp2(rm[...] - top)
    total = rl[...] * factor
    weighted = ro[...] * factor
    for j in range(NZ):
        factor = jnp.exp2(tops[j] - top)
        total = total + totals[j] * factor
        weighted = weighted + parts[j, 0:64, :].astype(F32) * factor
    attention = (weighted / total).astype(BF16)
    anchor = parts[meta[8], 80:96, :]
    for s in range(NZ):
        out[s, 0:64, :] = attention
        out[s, 64:80, :] = anchor


def merge(meta, parts, ro, rm, rl):
    return pl.pallas_call(
        merge_kernel,
        out_shape=jax.ShapeDtypeStruct((NZ, 80, HD), BF16),
        in_specs=[SMEM] + [VMEM] * 4,
        out_specs=VMEM,
        scratch_shapes=[pltpu.VMEM((HD, HD), F32)],
        compiler_params=params(),
        cost_estimate=cost(1 << 20, 1 << 19),
        name="merge",
    )(meta, parts, ro, rm, rl)


def picks_kernel(owner, out):
    y, c, x = lax.axis_index("y"), lax.axis_index("c"), lax.axis_index("x")
    col = iota((64, 256), 1)
    buf = col // 32
    slot = (
        lax.rem(col // 4, 8) * 8
        + lax.rem(y - lax.rem(buf, 4) + NY, NY) * NC
        + jnp.where(buf >= 4, 1 - c, c)
    )
    row = iota((64, 256), 0)
    same_step = lax.rem(col, 4) == row // 16
    request = lax.rem(row, 16)
    for s in range(NX):
        first = lax.rem(x + s, NX) * 16
        wanted = jnp.zeros((64, 256), jnp.int32)
        for j in range(16):
            wanted = jnp.where(request == j, owner[first + j], wanted)
        out[s] = ((wanted == slot) & same_step).astype(F32).astype(BF16)


def make_picks(owner):
    return pl.pallas_call(
        picks_kernel,
        out_shape=jax.ShapeDtypeStruct((NX, 64, 256), BF16),
        in_specs=[SMEM],
        out_specs=VMEM,
        compiler_params=params(),
        cost_estimate=cost(1 << 22, 1 << 18),
        name="picks",
    )(owner)


def line_product(w, bufs):
    total = jnp.zeros((128, HD), F32)
    for zz in range(NZ):
        left = jnp.concatenate([b[zz, 0:32, :] for b in bufs], axis=0)
        right = jnp.concatenate([b[zz, 32:64, :] for b in bufs], axis=0)
        total = total + dot(
            jnp.concatenate([left, right], axis=1), w[zz * 256 : (zz + 1) * 256, :]
        )
    high = total.astype(BF16)
    return high, (total - high.astype(F32)).astype(BF16)


def near_kernel(w, *refs):
    refs[4][0], refs[4][1] = line_product(w, refs[:4])


def project_near(w, bufs):
    return pl.pallas_call(
        near_kernel,
        out_shape=jax.ShapeDtypeStruct((2, 128, HD), BF16),
        in_specs=[VMEM] * 5,
        out_specs=VMEM,
        compiler_params=params(),
        cost_estimate=cost(1 << 26, 1 << 20),
        name="project_near",
    )(w, *bufs)


def project_kernel(picks, near, w, *refs):
    bufs, outs = refs[:4], refs[4:8]
    high, low = line_product(w, bufs)
    high = jnp.concatenate([near[0], high], axis=0)
    low = jnp.concatenate([near[1], low], axis=0)
    for s, out in enumerate(outs):
        out[...] = dot(picks[s], high) + dot(picks[s], low)


def project(picks, near, w, bufs):
    return pl.pallas_call(
        project_kernel,
        out_shape=(jax.ShapeDtypeStruct((64, HD), F32),) * 4,
        in_specs=[VMEM] * 7,
        out_specs=(VMEM,) * 4,
        compiler_params=params(),
        cost_estimate=cost(1 << 27, 2 << 20),
        name="project",
    )(picks, near, w, *bufs)


def places_kernel(*refs):
    meta, owner, lengths, blocks, sems = refs[3:]
    copies = [pltpu.make_async_copy(refs[i], refs[4 + i], sems.at[i]) for i in range(3)]
    for copy in copies:
        copy.start()
    for copy in copies:
        copy.wait()
    z, y, c = lax.axis_index("z"), lax.axis_index("y"), lax.axis_index("c")
    line = y * NC + c
    root = jnp.int32(0)
    for r in range(SLOTS):
        slot = owner[r]
        meta[jnp.where(slot & 7 == line, slot >> 3, 15)] = lengths[r]
        root = jnp.where(blocks[r] == 0, r, root)
    meta[8] = root // 8
    meta[9] = lax.rem(root, 8) // 2
    meta[10] = lax.rem(root, 2)
    meta[11] = jnp.where(root == z * 8 + line, 1, 0)


def find_places(*args):
    args = [pltpu.with_memory_space_constraint(a, pltpu.HBM) for a in args]
    return pl.pallas_call(
        places_kernel,
        out_shape=jax.ShapeDtypeStruct((16,), jnp.int32),
        in_specs=[pl.BlockSpec(memory_space=pltpu.HBM)] * 3,
        out_specs=SMEM,
        scratch_shapes=[pltpu.SMEM((SLOTS,), jnp.int32)] * 3 + [pltpu.SemaphoreType.DMA((3,))],
        compiler_params=params(),
        cost_estimate=cost(1 << 20, 1 << 19),
        name="places",
    )(*args)


def own_kernel(after, q, xk, xv, out, lse, values):
    causal = iota((128, 128), 0) >= iota((128, 128), 1)
    for k in range(2):
        values[k, :, 0:HD] = xv[:, k * HD : (k + 1) * HD]
        values[k, :, HD:] = jnp.ones((ROWS, HD), BF16)
    for group in range(4):
        units = [(group * 4 + h, half) for h in range(4) for half in range(2)]
        tiles, tops = [], []
        for h, half in units:
            near = (half + 1) * 128
            keys = xk[0:near, (h // 8) * HD : (h // 8 + 1) * HD]
            own = dot(q[near - 128 : near, h * HD : (h + 1) * HD], keys, NT)
            diagonal = jnp.where(causal, own[:, near - 128 :], LOW)
            tiles.append([own[:, :HD], diagonal] if half else [diagonal])
        for parts in tiles:
            tops.append(
                jnp.max(functools.reduce(jnp.maximum, parts), axis=1, keepdims=True) * SCALE2
            )
        for (h, half), parts, top in zip(units, tiles, tops):
            near = (half + 1) * 128
            weights = [jnp.exp2(t * SCALE2 - top).astype(BF16) for t in parts]
            weights = jnp.concatenate(weights, axis=1) if half else weights[0]
            summed = dot(weights, values[h // 8, 0:near, :])
            rows, lanes = slice(near - 128, near), slice(h * HD, (h + 1) * HD)
            out[rows, lanes] = summed[:, :HD] / summed[:, HD:]
            lse[rows, lanes] = top + jnp.log2(summed[:, HD:])


def context_own(after, q, xk, xv):
    return pl.pallas_call(
        own_kernel,
        out_shape=(jax.ShapeDtypeStruct((ROWS, 2048), F32),) * 2,
        in_specs=[VMEM] * 4,
        out_specs=(VMEM,) * 2,
        scratch_shapes=[pltpu.VMEM((2, ROWS, 2 * HD), BF16)],
        compiler_params=params(),
        cost_estimate=cost(1 << 30, 6 << 20, 1 << 20),
        name="context_own",
    )(after, q, xk, xv)


def far_kernel(meta, q, own, lse, *refs):
    bufs, (out, keys, values, staged, sems) = refs[:8], refs[8:]
    hide = jnp.where(meta[11] == 1, -LOW, 0.0).astype(F32)
    for k in range(2):
        values[k, :, HD:] = jnp.ones((ROWS, HD), BF16)
        for j, buf in enumerate(bufs):
            for half in range(2):
                at, tile = j * 32 + half * 16, k * 2 + half
                keys[k, at : at + 16, :] = buf[tile, 64:80, :]
                values[k, at : at + 16, 0:HD] = buf[4 + tile, 64:80, :]
    copies = []
    for group in range(4):
        k = group // 2
        heads = [slice(h * HD, (h + 1) * HD) for h in range(group * 4, group * 4 + 4)]
        scores = dot(jnp.concatenate([q[:, lanes] for lanes in heads], axis=0), keys[k], NT)
        tiles = [scores[i * ROWS : (i + 1) * ROWS] for i in range(4)]
        tops = [
            jnp.max(jnp.maximum(t[:, :HD], t[:, HD:]), axis=1, keepdims=True) * SCALE2 - hide
            for t in tiles
        ]
        nears = [lse[:, lanes] for lanes in heads]
        tops = [jnp.maximum(top, near) for top, near in zip(tops, nears)]
        weights = []
        for t, top in zip(tiles, tops):
            top = top + hide
            halves = [jnp.exp2(half * SCALE2 - top).astype(BF16) for half in (t[:, :HD], t[:, HD:])]
            weights.append(jnp.concatenate(halves, axis=1))
        summed = dot(jnp.concatenate(weights, axis=0), values[k])
        for i, (top, near, lanes) in enumerate(zip(tops, nears, heads)):
            part = summed[i * ROWS : (i + 1) * ROWS]
            factor = jnp.exp2(near - top)
            joint = part[:, :HD] + factor * own[:, lanes]
            staged[:, lanes] = (joint / (part[:, HD:] + factor)).astype(BF16)
        lanes = slice(group * 512, (group + 1) * 512)
        copies.append(pltpu.make_async_copy(staged.at[:, lanes], out.at[:, lanes], sems.at[group]))
        copies[-1].start()
    for copy in copies:
        copy.wait()


def context_far(meta, q, own, lse, bufs):
    return pl.pallas_call(
        far_kernel,
        out_shape=jax.ShapeDtypeStruct((ROWS, 2048), BF16),
        in_specs=[SMEM] + [VMEM] * 11,
        out_specs=pl.BlockSpec(memory_space=pl.ANY),
        scratch_shapes=[
            pltpu.VMEM((2, ROWS, HD), BF16),
            pltpu.VMEM((2, ROWS, 2 * HD), BF16),
            pltpu.VMEM((ROWS, 2048), BF16),
            pltpu.SemaphoreType.DMA((4,)),
        ],
        compiler_params=params(),
        cost_estimate=cost(1 << 30, 6 << 20, 1 << 20),
        name="context_far",
    )(meta, q, own, lse, *bufs)


def shifted(value, axis, size, shift):
    return lax.ppermute(value, axis, [(i, (i + shift) % size) for i in range(size)])


def on_device(
    ctx_queries,
    ctx_keys,
    ctx_values,
    block_map,
    cache_keys,
    cache_values,
    dec_queries,
    new_keys,
    new_values,
    cache_lengths,
    owner,
    out_weight,
):
    packed, *payloads = prep(
        dec_queries.reshape(STEPS, -1),
        new_keys.reshape(STEPS, -1),
        new_values.reshape(STEPS, -1),
        cache_keys,
        cache_values,
        ctx_keys,
        ctx_values,
    )
    shards = [shifted(payloads[s], "y", NY, s) for s in range(1, NY)]
    gathered = lax.all_to_all(packed, "z", 0, 0, tiled=True)
    meta = find_places(owner, cache_lengths, block_map)
    q, ro, rm, rl = line_part(gathered)
    q, ro, rm, rl, meta, *shards = lax.optimization_barrier((q, ro, rm, rl, meta, *shards))
    shards = [payloads[0]] + shards
    state = first_part(meta, q, shards)
    shards = shards + [shifted(b, "c", NC, 1) for b in shards]
    parts = lax.all_to_all(second_part(meta, q, state, shards), "z", 0, 0, tiled=True)
    merged = lax.all_to_all(merge(meta, parts, ro, rm, rl), "z", 0, 0, tiled=True)
    merged, owner = lax.optimization_barrier((merged, owner))
    picks = make_picks(owner)
    one, two, three = [shifted(merged, "y", NY, s) for s in range(1, NY)]
    own, lse = context_own(merged, ctx_queries, ctx_keys, ctx_values)
    own, lse, one = lax.optimization_barrier((own, lse, one))
    lines = [merged, one, two, three]
    swapped = [shifted(b, "c", NC, 1) for b in lines]
    near = project_near(out_weight, lines)
    mine, *others = project(picks, near, out_weight, swapped)
    ctx_out = context_far(meta, ctx_queries, own, lse, lines + swapped)
    total = mine
    for s, part in enumerate(others):
        total = total + shifted(part, "x", NX, s + 1)
    dec_out = total.astype(BF16).reshape(STEPS, 16, HD)
    return (ctx_out, dec_out)


def solution(mesh):
    grid = Mesh(mesh.devices.reshape(NZ, NY, NC, NX), ("z", "y", "c", "x"))
    ctx = ("z", "y", "c")
    in_specs = (
        P(ctx, "x"),
        P(ctx, "x"),
        P(ctx, "x"),
        P(),
        P(ctx, "x"),
        P(ctx, "x"),
        P(None, ctx, "x"),
        P(None, ctx, "x"),
        P(None, ctx, "x"),
        P(),
        P(),
        P("x", ctx),
    )
    out_specs = (P(ctx, "x"), P(None, "x", ctx))
    return jax.shard_map(on_device, mesh=grid, in_specs=in_specs, out_specs=out_specs, check_vma=False)
```

```python
import functools
import math

import jax
import jax.numpy as jnp
from jax import lax
from jax.experimental import pallas as pl
from jax.experimental.pallas import tpu as pltpu
from jax.sharding import Mesh, PartitionSpec as P

HD = 128
STEPS = 4
NZ, NY, NC, NX = 8, 4, 2, 4
ROWS = 256
SLOTS = 64
SCALE2 = math.log2(math.e) / math.sqrt(HD)
LOW = -1e29
FLOOR = -(2.0**80)
F32 = jnp.float32
BF16 = jnp.bfloat16
VMEM = pl.BlockSpec(memory_space=pltpu.VMEM)
SMEM = pl.BlockSpec(memory_space=pltpu.SMEM)
NT = (((1,), (1,)), ((), ()))
NN = (((1,), (0,)), ((), ()))


def iota(shape, dim):
    return lax.broadcasted_iota(jnp.int32, shape, dim)


def dot(a, b, dims=NN):
    return lax.dot_general(a, b, dims, preferred_element_type=F32)


def params(mib=16):
    return pltpu.CompilerParams(vmem_limit_bytes=mib * 2**20)


def cost(flops, moved, trans=0):
    return pl.CostEstimate(flops=flops, bytes_accessed=moved, transcendentals=trans)


def prep_kernel(dq, nk, nv, ck, cv, xk, xv, q_out, p0, p1, p2, p3, scratch, dq_v, nk_v, nv_v, xk_v, xv_v, sems):
    y = lax.axis_index("y")
    copies = [
        (dq, dq_v),
        (nk, nk_v),
        (nv, nv_v),
        (ck, p0.at[0:ROWS, :]),
        (cv, p0.at[ROWS : 2 * ROWS, :]),
        (xk, xk_v),
        (xv, xv_v),
    ]
    copies = [pltpu.make_async_copy(src, dst, sems.at[i]) for i, (src, dst) in enumerate(copies)]
    for copy in copies:
        copy.start()
    scratch[...] = jnp.zeros_like(scratch)
    row, col = iota((80, 160), 0), iota((80, 160), 1)
    pick = (col == (row // 4) * 8 + row % 4).astype(F32).astype(BF16)
    for copy in copies[:3]:
        copy.wait()
    for h in range(16):
        scratch[h * 8 : h * 8 + 4, :] = dq_v[:, h * HD : (h + 1) * HD].astype(F32)
    for i, ref in enumerate((nk_v, nv_v)):
        for k in range(2):
            at = 128 + (i * 2 + k) * 8
            scratch[at : at + 4, :] = ref[:, k * HD : (k + 1) * HD].astype(F32)
    packed = dot(pick, scratch[...].astype(BF16)).astype(BF16)
    for s in range(NZ):
        q_out[s] = packed
    for copy in copies[3:]:
        copy.wait()
    shard = p0[0 : 2 * ROWS, :]
    for out in (p1, p2, p3):
        out[0 : 2 * ROWS, :] = shard
    for s, out in enumerate((p0, p1, p2, p3)):
        for i in range(8):
            source, k = (xk_v, xv_v)[i // 4], (i % 4) // 2
            for core in range(2):
                at = lax.rem(y + s, NY) * 64 + core * 32 + (i % 2) * 16
                tile = source[pl.ds(pl.multiple_of(at, 16), 16), k * HD : (k + 1) * HD]
                out[512 + i * 16 : 528 + i * 16, core * HD : (core + 1) * HD] = tile


def prep(*args):
    args = [pltpu.with_memory_space_constraint(a, pltpu.HBM) for a in args]
    payload = jax.ShapeDtypeStruct((640, 256), BF16)
    return pl.pallas_call(
        prep_kernel,
        out_shape=(jax.ShapeDtypeStruct((NZ, 80, HD), BF16),) + (payload,) * 4,
        in_specs=[pl.BlockSpec(memory_space=pltpu.HBM)] * 7,
        out_specs=(VMEM,) * 5,
        scratch_shapes=[
            pltpu.VMEM((160, HD), F32),
            pltpu.VMEM((STEPS, 2048), BF16),
            pltpu.VMEM((STEPS, 256), BF16),
            pltpu.VMEM((STEPS, 256), BF16),
            pltpu.VMEM((ROWS, 256), BF16),
            pltpu.VMEM((ROWS, 256), BF16),
            pltpu.SemaphoreType.DMA((7,)),
        ],
        compiler_params=params(),
        cost_estimate=cost(1 << 20, 1 << 20),
        name="prep",
    )(*args)


def line_kernel(g, q_out, ro_out, rm_out, rl_out):
    z = lax.axis_index("z")
    row, col = iota((256, 256), 0), iota((256, 256), 1)
    source = lax.rem(row // 4, 8) * 32 + (row // 32) * 4 + lax.rem(row, 4)
    pick = (col == source).astype(F32).astype(BF16)
    for k in range(2):
        natural = jnp.concatenate([g[s, k * 32 : (k + 1) * 32, :] for s in range(NZ)], axis=0)
        q_out[k * 256 : (k + 1) * 256, :] = dot(pick, natural).astype(BF16)
    mine = q_out[pl.ds(pl.multiple_of(z * 64, 64), 64), :]
    tokens = jnp.concatenate([g[s, 64:80, :] for s in range(NZ)], axis=0)
    wide = tokens.astype(F32)
    values = jnp.concatenate([wide[8:], wide[:8]], axis=0).astype(BF16)
    scores = dot(mine, tokens, NT) * SCALE2
    row, col = iota((64, 128), 0), iota((64, 128), 1)
    seen = (
        (lax.rem(row // 4, 8) == col // 16)
        & (lax.rem(col, 16) // 4 == z // 4)
        & (lax.rem(col, 4) <= lax.rem(row, 4))
    )
    scores = jnp.where(seen, scores, LOW)
    top = jnp.max(scores, axis=1, keepdims=True)
    weights = jnp.exp2(scores - top)
    rm_out[...] = jnp.broadcast_to(top, (64, HD))
    rl_out[...] = jnp.broadcast_to(jnp.sum(weights, axis=1, keepdims=True), (64, HD))
    ro_out[...] = dot(weights.astype(BF16), values)


def line_part(gathered):
    part = jax.ShapeDtypeStruct((64, HD), F32)
    return pl.pallas_call(
        line_kernel,
        out_shape=(jax.ShapeDtypeStruct((512, HD), BF16), part, part, part),
        in_specs=[VMEM],
        out_specs=(VMEM,) * 4,
        compiler_params=params(),
        cost_estimate=cost(1 << 24, 1 << 20),
        name="line_part",
    )(gathered)


def shard_scores(meta, q, bufs, k, core, scores):
    z, y = lax.axis_index("z"), lax.axis_index("y")
    rowslot = iota((32, HD), 0) // 4
    length = jnp.zeros((32, HD), jnp.int32)
    for s in range(8):
        length = jnp.where(rowslot == s, meta[s], length)
    lane = iota((32, HD), 1)
    tops = []
    for b in range(4):
        room = length - (z * 8 + lax.rem(y - b + NY, NY) * NC + core) * ROWS
        keep = jnp.concatenate([lane < room, lane + HD < room], axis=1)
        raw = dot(q[k * 256 : (k + 1) * 256, :], bufs[b][0:ROWS, k * HD : (k + 1) * HD], NT)
        raw = jnp.where(keep[None], raw.reshape(8, 32, 256), LOW).reshape(256, 256)
        scores[k, b] = raw
        tops.append(jnp.max(jnp.maximum(raw[:, :HD], raw[:, HD:]), axis=1, keepdims=True))
    return tops


def shard_sums(bufs, k, tops, top, scores, total, weighted):
    for b in range(4):
        weights = jnp.exp2((scores[k, b] - tops[b]) * SCALE2)
        factor = jnp.exp2(tops[b] * SCALE2 - top)
        total = total + (weights[:, :HD] + weights[:, HD:]) * factor
        weighted = weighted + factor * dot(
            weights.astype(BF16), bufs[b][ROWS : 2 * ROWS, k * HD : (k + 1) * HD]
        )
    return total, weighted


def first_kernel(meta, q, *refs):
    bufs, (o_out, m_out, l_out, scores) = refs[:4], refs[4:]
    core = lax.axis_index("c")
    tops = [shard_scores(meta, q, bufs, k, core, scores) for k in range(2)]
    zeros = jnp.zeros((256, HD), F32)
    for k in range(2):
        rows = slice(k * 256, (k + 1) * 256)
        top = jnp.maximum(functools.reduce(jnp.maximum, tops[k]) * SCALE2, FLOOR)
        l_out[rows, :], o_out[rows, :] = shard_sums(bufs, k, tops[k], top, scores, zeros, zeros)
        m_out[rows, :] = jnp.broadcast_to(top, (256, HD))


def first_part(meta, q, bufs):
    part = jax.ShapeDtypeStruct((512, HD), F32)
    return pl.pallas_call(
        first_kernel,
        out_shape=(part,) * 3,
        in_specs=[SMEM] + [VMEM] * 5,
        out_specs=(VMEM,) * 3,
        scratch_shapes=[pltpu.VMEM((2, 4, 256, 256), F32)],
        compiler_params=params(),
        cost_estimate=cost(1 << 29, 2 << 20, 1 << 19),
        name="first_part",
    )(meta, q, *bufs)


def second_kernel(meta, q, o, m, l, *refs):
    all_bufs, bufs, (out, scores) = refs[:8], refs[4:8], refs[8:]
    core = 1 - lax.axis_index("c")
    tops = [shard_scores(meta, q, bufs, k, core, scores) for k in range(2)]
    column = iota((256, HD), 1)
    for k in range(2):
        rows = slice(k * 256, (k + 1) * 256)
        top = jnp.maximum(functools.reduce(jnp.maximum, tops[k]) * SCALE2, m[rows, :])
        top = top.astype(BF16).astype(F32)
        factor = jnp.exp2(m[rows, :] - top)
        total, weighted = shard_sums(
            bufs, k, tops[k], top, scores, l[rows, :] * factor, o[rows, :] * factor
        )
        total = jnp.sum(total, axis=1, keepdims=True)
        total_high = total.astype(BF16).astype(F32)
        total_low = total - total_high
        stats = jnp.where(
            column == 0, top, jnp.where(column == 1, total_high, jnp.where(column == 2, total_low, 0.0))
        )
        weighted = weighted.astype(BF16)
        for pair in range(2):
            flipped = jnp.transpose(stats[pair * 128 : (pair + 1) * 128])[:16].astype(BF16)
            out[k * 4 + pair * 2, 64:80, :] = flipped
            out[k * 4 + pair * 2 + 1, 64:80, :] = flipped
        for part in range(4):
            out[k * 4 + part, 0:64, :] = weighted[part * 64 : (part + 1) * 64]
    y, c = lax.axis_index("y"), lax.axis_index("c")
    root_shift = lax.rem(y - meta[9] + NY, NY)
    for b in range(8):
        for lane_half in range(2):
            swapped = b // 4
            from_core = jnp.where(meta[10] == c, 0, 1)

            @pl.when((root_shift == b % 4) & (from_core == swapped) & (c == lane_half))
            def _(b=b, lane_half=lane_half):
                lanes = slice(lane_half * HD, (lane_half + 1) * HD)
                for piece in range(NZ):
                    out[piece, 80:96, :] = all_bufs[b][512 + piece * 16 : 528 + piece * 16, lanes]


def second_part(meta, q, state, bufs):
    return pl.pallas_call(
        second_kernel,
        out_shape=jax.ShapeDtypeStruct((NZ, 96, HD), BF16),
        in_specs=[SMEM] + [VMEM] * 12,
        out_specs=VMEM,
        scratch_shapes=[pltpu.VMEM((2, 4, 256, 256), F32)],
        compiler_params=params(),
        cost_estimate=cost(1 << 29, 2 << 20, 1 << 19),
        name="second_part",
    )(meta, q, *state, *bufs)


def merge_kernel(meta, parts, ro, rm, rl, out, scratch):
    z = lax.axis_index("z")
    stats = jnp.concatenate([parts[j, 64:80, :] for j in range(NZ)], axis=0).astype(F32)
    scratch[...] = jnp.transpose(stats)
    mine = scratch[pl.ds(pl.multiple_of(lax.rem(z, 2) * 64, 64), 64), :]
    tops = [mine[:, j * 16 : j * 16 + 1] for j in range(NZ)]
    totals = [mine[:, j * 16 + 1 : j * 16 + 2] + mine[:, j * 16 + 2 : j * 16 + 3] for j in range(NZ)]
    top = rm[...]
    for t in tops:
        top = jnp.maximum(top, t)
    factor = jnp.exp2(rm[...] - top)
    total = rl[...] * factor
    weighted = ro[...] * factor
    for j in range(NZ):
        factor = jnp.exp2(tops[j] - top)
        total = total + totals[j] * factor
        weighted = weighted + parts[j, 0:64, :].astype(F32) * factor
    attention = (weighted / total).astype(BF16)
    anchor = parts[meta[8], 80:96, :]
    for s in range(NZ):
        out[s, 0:64, :] = attention
        out[s, 64:80, :] = anchor


def merge(meta, parts, ro, rm, rl):
    return pl.pallas_call(
        merge_kernel,
        out_shape=jax.ShapeDtypeStruct((NZ, 80, HD), BF16),
        in_specs=[SMEM] + [VMEM] * 4,
        out_specs=VMEM,
        scratch_shapes=[pltpu.VMEM((HD, HD), F32)],
        compiler_params=params(),
        cost_estimate=cost(1 << 20, 1 << 19),
        name="merge",
    )(meta, parts, ro, rm, rl)


def picks_kernel(owner, out):
    y, c, x = lax.axis_index("y"), lax.axis_index("c"), lax.axis_index("x")
    col = iota((64, 256), 1)
    buf = col // 32
    slot = (
        lax.rem(col // 4, 8) * 8
        + lax.rem(y - lax.rem(buf, 4) + NY, NY) * NC
        + jnp.where(buf >= 4, 1 - c, c)
    )
    row = iota((64, 256), 0)
    same_step = lax.rem(col, 4) == row // 16
    request = lax.rem(row, 16)
    for s in range(NX):
        first = lax.rem(x + s, NX) * 16
        wanted = jnp.zeros((64, 256), jnp.int32)
        for j in range(16):
            wanted = jnp.where(request == j, owner[first + j], wanted)
        out[s] = ((wanted == slot) & same_step).astype(F32).astype(BF16)


def make_picks(owner):
    return pl.pallas_call(
        picks_kernel,
        out_shape=jax.ShapeDtypeStruct((NX, 64, 256), BF16),
        in_specs=[SMEM],
        out_specs=VMEM,
        compiler_params=params(),
        cost_estimate=cost(1 << 22, 1 << 18),
        name="picks",
    )(owner)


def line_product(w, bufs):
    total = jnp.zeros((128, HD), F32)
    for zz in range(NZ):
        left = jnp.concatenate([b[zz, 0:32, :] for b in bufs], axis=0)
        right = jnp.concatenate([b[zz, 32:64, :] for b in bufs], axis=0)
        total = total + dot(
            jnp.concatenate([left, right], axis=1), w[zz * 256 : (zz + 1) * 256, :]
        )
    high = total.astype(BF16)
    return high, (total - high.astype(F32)).astype(BF16)


def near_kernel(w, *refs):
    refs[4][0], refs[4][1] = line_product(w, refs[:4])


def project_near(w, bufs):
    return pl.pallas_call(
        near_kernel,
        out_shape=jax.ShapeDtypeStruct((2, 128, HD), BF16),
        in_specs=[VMEM] * 5,
        out_specs=VMEM,
        compiler_params=params(),
        cost_estimate=cost(1 << 26, 1 << 20),
        name="project_near",
    )(w, *bufs)


def project_kernel(picks, near, w, *refs):
    bufs, outs = refs[:4], refs[4:8]
    high, low = line_product(w, bufs)
    high = jnp.concatenate([near[0], high], axis=0)
    low = jnp.concatenate([near[1], low], axis=0)
    for s, out in enumerate(outs):
        out[...] = dot(picks[s], high) + dot(picks[s], low)


def project(picks, near, w, bufs):
    return pl.pallas_call(
        project_kernel,
        out_shape=(jax.ShapeDtypeStruct((64, HD), F32),) * 4,
        in_specs=[VMEM] * 7,
        out_specs=(VMEM,) * 4,
        compiler_params=params(),
        cost_estimate=cost(1 << 27, 2 << 20),
        name="project",
    )(picks, near, w, *bufs)


def places_kernel(*refs):
    meta, owner, lengths, blocks, sems = refs[3:]
    copies = [pltpu.make_async_copy(refs[i], refs[4 + i], sems.at[i]) for i in range(3)]
    for copy in copies:
        copy.start()
    for copy in copies:
        copy.wait()
    z, y, c = lax.axis_index("z"), lax.axis_index("y"), lax.axis_index("c")
    line = y * NC + c
    root = jnp.int32(0)
    for r in range(SLOTS):
        slot = owner[r]
        meta[jnp.where(slot & 7 == line, slot >> 3, 15)] = lengths[r]
        root = jnp.where(blocks[r] == 0, r, root)
    meta[8] = root // 8
    meta[9] = lax.rem(root, 8) // 2
    meta[10] = lax.rem(root, 2)
    meta[11] = jnp.where(root == z * 8 + line, 1, 0)


def find_places(*args):
    args = [pltpu.with_memory_space_constraint(a, pltpu.HBM) for a in args]
    return pl.pallas_call(
        places_kernel,
        out_shape=jax.ShapeDtypeStruct((16,), jnp.int32),
        in_specs=[pl.BlockSpec(memory_space=pltpu.HBM)] * 3,
        out_specs=SMEM,
        scratch_shapes=[pltpu.SMEM((SLOTS,), jnp.int32)] * 3 + [pltpu.SemaphoreType.DMA((3,))],
        compiler_params=params(),
        cost_estimate=cost(1 << 20, 1 << 19),
        name="places",
    )(*args)


def own_kernel(after, q, xk, xv, out, lse, values):
    causal = iota((128, 128), 0) >= iota((128, 128), 1)
    for k in range(2):
        values[k, :, 0:HD] = xv[:, k * HD : (k + 1) * HD]
        values[k, :, HD:] = jnp.ones((ROWS, HD), BF16)
    for group in range(4):
        units = [(group * 4 + h, half) for h in range(4) for half in range(2)]
        tiles, tops = [], []
        for h, half in units:
            near = (half + 1) * 128
            keys = xk[0:near, (h // 8) * HD : (h // 8 + 1) * HD]
            own = dot(q[near - 128 : near, h * HD : (h + 1) * HD], keys, NT)
            diagonal = jnp.where(causal, own[:, near - 128 :], LOW)
            tiles.append([own[:, :HD], diagonal] if half else [diagonal])
        for parts in tiles:
            tops.append(
                jnp.max(functools.reduce(jnp.maximum, parts), axis=1, keepdims=True) * SCALE2
            )
        for (h, half), parts, top in zip(units, tiles, tops):
            near = (half + 1) * 128
            weights = [jnp.exp2(t * SCALE2 - top).astype(BF16) for t in parts]
            weights = jnp.concatenate(weights, axis=1) if half else weights[0]
            summed = dot(weights, values[h // 8, 0:near, :])
            rows, lanes = slice(near - 128, near), slice(h * HD, (h + 1) * HD)
            out[rows, lanes] = summed[:, :HD] / summed[:, HD:]
            lse[rows, lanes] = top + jnp.log2(summed[:, HD:])


def context_own(after, q, xk, xv):
    return pl.pallas_call(
        own_kernel,
        out_shape=(jax.ShapeDtypeStruct((ROWS, 2048), F32),) * 2,
        in_specs=[VMEM] * 4,
        out_specs=(VMEM,) * 2,
        scratch_shapes=[pltpu.VMEM((2, ROWS, 2 * HD), BF16)],
        compiler_params=params(),
        cost_estimate=cost(1 << 30, 6 << 20, 1 << 20),
        name="context_own",
    )(after, q, xk, xv)


def far_kernel(meta, q, own, lse, *refs):
    bufs, (out, keys, values, staged, sems) = refs[:8], refs[8:]
    hide = jnp.where(meta[11] == 1, -LOW, 0.0).astype(F32)
    for k in range(2):
        values[k, :, HD:] = jnp.ones((ROWS, HD), BF16)
        for j, buf in enumerate(bufs):
            for half in range(2):
                at, tile = j * 32 + half * 16, k * 2 + half
                keys[k, at : at + 16, :] = buf[tile, 64:80, :]
                values[k, at : at + 16, 0:HD] = buf[4 + tile, 64:80, :]
    copies = []
    for group in range(4):
        k = group // 2
        heads = [slice(h * HD, (h + 1) * HD) for h in range(group * 4, group * 4 + 4)]
        scores = dot(jnp.concatenate([q[:, lanes] for lanes in heads], axis=0), keys[k], NT)
        tiles = [scores[i * ROWS : (i + 1) * ROWS] for i in range(4)]
        tops = [
            jnp.max(jnp.maximum(t[:, :HD], t[:, HD:]), axis=1, keepdims=True) * SCALE2 - hide
            for t in tiles
        ]
        nears = [lse[:, lanes] for lanes in heads]
        tops = [jnp.maximum(top, near) for top, near in zip(tops, nears)]
        weights = []
        for t, top in zip(tiles, tops):
            top = top + hide
            halves = [jnp.exp2(half * SCALE2 - top).astype(BF16) for half in (t[:, :HD], t[:, HD:])]
            weights.append(jnp.concatenate(halves, axis=1))
        summed = dot(jnp.concatenate(weights, axis=0), values[k])
        for i, (top, near, lanes) in enumerate(zip(tops, nears, heads)):
            part = summed[i * ROWS : (i + 1) * ROWS]
            factor = jnp.exp2(near - top)
            joint = part[:, :HD] + factor * own[:, lanes]
            staged[:, lanes] = (joint / (part[:, HD:] + factor)).astype(BF16)
        lanes = slice(group * 512, (group + 1) * 512)
        copies.append(pltpu.make_async_copy(staged.at[:, lanes], out.at[:, lanes], sems.at[group]))
        copies[-1].start()
    for copy in copies:
        copy.wait()


def context_far(meta, q, own, lse, bufs):
    return pl.pallas_call(
        far_kernel,
        out_shape=jax.ShapeDtypeStruct((ROWS, 2048), BF16),
        in_specs=[SMEM] + [VMEM] * 11,
        out_specs=pl.BlockSpec(memory_space=pl.ANY),
        scratch_shapes=[
            pltpu.VMEM((2, ROWS, HD), BF16),
            pltpu.VMEM((2, ROWS, 2 * HD), BF16),
            pltpu.VMEM((ROWS, 2048), BF16),
            pltpu.SemaphoreType.DMA((4,)),
        ],
        compiler_params=params(),
        cost_estimate=cost(1 << 30, 6 << 20, 1 << 20),
        name="context_far",
    )(meta, q, own, lse, *bufs)


def shifted(value, axis, size, shift):
    return lax.ppermute(value, axis, [(i, (i + shift) % size) for i in range(size)])


def on_device(
    ctx_queries,
    ctx_keys,
    ctx_values,
    block_map,
    cache_keys,
    cache_values,
    dec_queries,
    new_keys,
    new_values,
    cache_lengths,
    owner,
    out_weight,
):
    packed, *payloads = prep(
        dec_queries.reshape(STEPS, -1),
        new_keys.reshape(STEPS, -1),
        new_values.reshape(STEPS, -1),
        cache_keys,
        cache_values,
        ctx_keys,
        ctx_values,
    )
    shards = [shifted(payloads[s], "y", NY, s) for s in range(1, NY)]
    gathered = lax.all_to_all(packed, "z", 0, 0, tiled=True)
    meta = find_places(owner, cache_lengths, block_map)
    q, ro, rm, rl = line_part(gathered)
    q, ro, rm, rl, meta, *shards = lax.optimization_barrier((q, ro, rm, rl, meta, *shards))
    shards = [payloads[0]] + shards
    state = first_part(meta, q, shards)
    shards = shards + [shifted(b, "c", NC, 1) for b in shards]
    parts = lax.all_to_all(second_part(meta, q, state, shards), "z", 0, 0, tiled=True)
    merged = lax.all_to_all(merge(meta, parts, ro, rm, rl), "z", 0, 0, tiled=True)
    merged, owner = lax.optimization_barrier((merged, owner))
    picks = make_picks(owner)
    one, two, three = [shifted(merged, "y", NY, s) for s in range(1, NY)]
    own, lse = context_own(merged, ctx_queries, ctx_keys, ctx_values)
    own, lse, picks, one = lax.optimization_barrier((own, lse, picks, one))
    lines = [merged, one, two, three]
    swapped = [shifted(b, "c", NC, 1) for b in lines]
    near = project_near(out_weight, lines)
    mine, *others = project(picks, near, out_weight, swapped)
    ctx_out = context_far(meta, ctx_queries, own, lse, lines + swapped)
    total = mine
    for s, part in reversed(list(enumerate(others))):
        total = total + shifted(part, "x", NX, s + 1)
    dec_out = total.astype(BF16).reshape(STEPS, 16, HD)
    return (ctx_out, dec_out)


def solution(mesh):
    grid = Mesh(mesh.devices.reshape(NZ, NY, NC, NX), ("z", "y", "c", "x"))
    ctx = ("z", "y", "c")
    in_specs = (
        P(ctx, "x"),
        P(ctx, "x"),
        P(ctx, "x"),
        P(),
        P(ctx, "x"),
        P(ctx, "x"),
        P(None, ctx, "x"),
        P(None, ctx, "x"),
        P(None, ctx, "x"),
        P(),
        P(),
        P("x", ctx),
    )
    out_specs = (P(ctx, "x"), P(None, "x", ctx))
    return jax.shard_map(on_device, mesh=grid, in_specs=in_specs, out_specs=out_specs, check_vma=False)
```
